512 devices in a mesh: leaf: 32 (over z, core), sub: 16 (over y, x).
Axes of the slice: x: 4, y: 4, z: 16, core: 2. Of those that a mesh axis runs over, the one named last changes fastest.
Arguments:
- sources: float32 [16, 524288], P(None, ('leaf', 'sub')), may hold values from -6 to 6
- points: float32 [3, 524288], P(None, ('leaf', 'sub')), may hold values from -1 to 1
- basis: float32 [4096, 64, 128], P(('leaf', 'sub')), may hold values from -0.5 to 0.5
- leaf_transfer: float32 [4096, 4096], P(('leaf', 'sub')), may hold values from -1 to 1
- dev_transfer: float32 [512, 4096], P(('leaf', 'sub')), may hold values from -1 to 1
- leaf_coupling: float32 [4096, 8, 4096], P(('leaf', 'sub')), may hold values from -0.25 to 0.25
- dev_coupling: float32 [512, 8, 4096], P(('leaf', 'sub')), may hold values from -0.25 to 0.25
- grp_coupling: float32 [32, 8, 4096], P('leaf'), may hold values from -0.25 to 0.25
- near_list: int32 [4096, 8], P(('leaf', 'sub')), may hold values from 0 to 127
- leaf_far: int32 [4096, 8], P(('leaf', 'sub')), may hold values from 0 to 127
- dev_far: int32 [512, 8], P(('leaf', 'sub')), may hold values from 0 to 511
- grp_far: int32 [32, 8], P('leaf'), may hold values from 0 to 31
Outputs:
- product: float32 [16, 524288], P(None, ('leaf', 'sub'))
The draws below stay inside these ranges and needn't reach their ends.
Inputs may be any that keep to these rules, and one draw needn't show every extreme that they name: Leaf numbers in near_list and leaf_far count within the subtree of the leaf that lists them; entries may repeat. `leaf_far`: entries may repeat. `dev_far`: entries may repeat. `grp_far`: entries may repeat.
All inputs are finite; a program needn't handle non-finite values.
Results may differ from the reference program's by a relative error of at most 0.0001.
Values sent between devices are 32-bit elements; how exact they have to be, the bound alone decides.
A program may use at most 64 MiB of HBM per device.

```python
import math
import jax
import jax.numpy as jnp
from jax import lax

LEAF = 128
RANK = 64
NVEC = 16
NEAR = 8
FAR_LEAF = 8
FAR_DEV = 8
FAR_GRP = 8
LEAF_DEV = 8
LEAVES = 4096
NPTS = 524288
GROUP_LEAVES = 128
N_LEAF = 32
N_SUB = 16


def set_ends(values, own_key, smallest, high):
    dims = values.shape
    index_at = [jax.random.randint(jax.random.fold_in(own_key, axis), (), 0, dims[axis]) for axis in range(len(dims))]
    values = values.at[tuple(index_at)].set(smallest)
    longest = dims.index(max(dims))
    index_at[longest] = (index_at[longest] + 1) % dims[longest]
    return values.at[tuple(index_at)].set(high)


def level_of(own_key, dims, cuts, low, top_value):
    def one(dim, parts):
        heights = jax.random.uniform(jax.random.fold_in(jax.random.fold_in(own_key, 6), dim), (parts,), jnp.float32, low / len(cuts), top_value / len(cuts))
        return jnp.repeat(jnp.exp(heights), dims[dim] // parts).reshape((-1,) + (1,) * (len(dims) - dim - 1))

    level = one(*cuts[0])
    for cut in cuts[1:]:
        level = level * one(*cut)
    return level


def normal_values(own_key, dims, spread, most, shards=(), kind=jnp.bfloat16):
    entries = jax.random.normal(own_key, dims, jnp.float32) * spread
    if len(shards) > 0:
        entries = level_of(own_key, dims, shards, -0.22, 0.18) * entries
    return jnp.clip(entries, min=-most, max=most).astype(kind)


def setup_inputs(seed: int = 0) -> dict:
    splits = jax.random.split(jax.random.key(seed), 13)
    return {
        "sources": normal_values(splits[0], (NVEC, NPTS), 1.0, 6.0, ((1, 512),), jnp.float32),
        "points": jnp.clip(jax.random.uniform(splits[1], (3, NPTS), jnp.float32, -1.0, 1.0) * level_of(splits[1], (3, NPTS), ((1, 512),), -0.4, 0.0), -1.0, 1.0),
        "basis": normal_values(splits[2], (LEAVES, RANK, LEAF), LEAF ** -0.5, 0.5, ((0, 512),), jnp.float32),
        "leaf_transfer": normal_values(splits[3], (LEAVES, RANK * RANK), 0.0625, 1.0, ((0, 512),), jnp.float32),
        "dev_transfer": normal_values(splits[4], (N_LEAF * N_SUB, RANK * RANK), 0.0625, 1.0, ((0, 512),), jnp.float32),
        "leaf_coupling": normal_values(splits[5], (LEAVES, FAR_LEAF, RANK * RANK), (RANK * FAR_LEAF) ** -0.5, 0.25, ((0, 512),), jnp.float32),
        "dev_coupling": normal_values(splits[6], (N_LEAF * N_SUB, FAR_DEV, RANK * RANK), (RANK * FAR_DEV) ** -0.5, 0.25, ((0, 512),), jnp.float32),
        "grp_coupling": normal_values(splits[7], (N_LEAF, FAR_GRP, RANK * RANK), (RANK * FAR_GRP) ** -0.5, 0.25, ((0, 32),), jnp.float32),
        "near_list": set_ends(jax.random.randint(splits[8], (LEAVES, NEAR), 0, GROUP_LEAVES), jax.random.fold_in(splits[8], 1), 0, GROUP_LEAVES - 1).astype(jnp.int32),
        "leaf_far": set_ends(jax.random.randint(splits[9], (LEAVES, FAR_LEAF), 0, GROUP_LEAVES), jax.random.fold_in(splits[9], 1), 0, GROUP_LEAVES - 1).astype(jnp.int32),
        "dev_far": set_ends(jax.random.randint(splits[10], (N_LEAF * N_SUB, FAR_DEV), 0, N_LEAF * N_SUB), jax.random.fold_in(splits[10], 1), 0, (N_LEAF * N_SUB) - 1).astype(jnp.int32),
        "grp_far": set_ends(jax.random.randint(splits[11], (N_LEAF, FAR_GRP), 0, N_LEAF), jax.random.fold_in(splits[11], 1), 0, N_LEAF - 1).astype(jnp.int32),
    }


delta_sq = 0.01

def kernel_block(targets, sources):
    along_x = targets[0][:, :, None] - sources[0][:, None, :]
    along_y = targets[1][:, :, None] - sources[1][:, None, :]
    along_z = targets[2][:, :, None] - sources[2][:, None, :]
    return 1.0 / jnp.sqrt(along_x * along_x + along_y * along_y + along_z * along_z + delta_sq)

def reference(sources, points, basis, leaf_transfer, dev_transfer, leaf_coupling, dev_coupling, grp_coupling, near_list, leaf_far, dev_far, grp_far):
    highest = lax.Precision.HIGHEST
    devices = N_LEAF * N_SUB
    leaves = devices * LEAF_DEV
    per_group = LEAF_DEV * N_SUB
    signal = sources.reshape(NVEC, leaves, LEAF)
    leaf_coef = jnp.einsum('tal,vtl->tva', basis, signal, precision=highest)
    leaf_maps = leaf_transfer.reshape(devices, LEAF_DEV, RANK, RANK)
    dev_coef = jnp.einsum('dtab,dtvb->dva', leaf_maps, leaf_coef.reshape(devices, LEAF_DEV, NVEC, RANK), precision=highest)
    dev_maps = dev_transfer.reshape(N_LEAF, N_SUB, RANK, RANK)
    grp_coef = jnp.einsum('gsab,gsvb->gva', dev_maps, dev_coef.reshape(N_LEAF, N_SUB, NVEC, RANK), precision=highest)
    grp_local = jnp.einsum('gkab,gkvb->gva', grp_coupling.reshape(N_LEAF, FAR_GRP, RANK, RANK), grp_coef[grp_far], precision=highest)
    dev_local = jnp.einsum('dkab,dkvb->dva', dev_coupling.reshape(devices, FAR_DEV, RANK, RANK), dev_coef[dev_far], precision=highest)
    dev_total = dev_local + jnp.einsum('gsab,gva->gsvb', dev_maps, grp_local, precision=highest).reshape(devices, NVEC, RANK)
    near_weight = 1.0 / math.sqrt(NEAR * LEAF)

    def one_group(pieces):
        g_coef, g_signal, g_points, g_basis, g_maps, g_coupling, g_near, g_far, g_total = pieces
        far_local = jnp.einsum('tkab,tkvb->tva', g_coupling.reshape(per_group, FAR_LEAF, RANK, RANK), g_coef[g_far], precision=highest)
        leaf_total = far_local + jnp.einsum('tab,tva->tvb', g_maps.reshape(per_group, RANK, RANK), g_total, precision=highest)
        far_field = jnp.einsum('tal,tva->tvl', g_basis, leaf_total, precision=highest)

        def near_step(position, running):
            source_leaves = lax.dynamic_index_in_dim(g_near, position, 1, keepdims=False)
            kernel_tile = kernel_block(g_points, g_points[:, source_leaves, :])
            return running + jnp.einsum('tpq,vtq->tvp', kernel_tile, g_signal[:, source_leaves, :], precision=highest)
        near_field = lax.fori_loop(0, NEAR, near_step, jnp.zeros((per_group, NVEC, LEAF), jnp.float32))
        return far_field + near_weight * near_field
    outputs = lax.map(one_group, (leaf_coef.reshape(N_LEAF, per_group, NVEC, RANK), signal.reshape(NVEC, N_LEAF, per_group, LEAF).transpose(1, 0, 2, 3), points.reshape(3, N_LEAF, per_group, LEAF).transpose(1, 0, 2, 3), basis.reshape(N_LEAF, per_group, RANK, LEAF), leaf_transfer.reshape(N_LEAF, per_group, RANK * RANK), leaf_coupling.reshape(N_LEAF, per_group, FAR_LEAF, RANK * RANK), near_list.reshape(N_LEAF, per_group, NEAR), leaf_far.reshape(N_LEAF, per_group, FAR_LEAF), jnp.repeat(dev_total, LEAF_DEV, axis=0).reshape(N_LEAF, per_group, NVEC, RANK)))
    return outputs.reshape(leaves, NVEC, LEAF).transpose(1, 0, 2).reshape(NVEC, leaves * LEAF)
```

```python
import jax
import jax.numpy as jnp
from jax import lax
from jax.experimental import pallas as pl
from jax.experimental.pallas import tpu as pltpu
from jax.sharding import PartitionSpec as P

MESH = pl.DeviceIdType.MESH
F32, BF16 = jnp.float32, jnp.bfloat16
DELTA_SQ = 0.01
NZ, NSUB, SIDE = 16, 16, 4
LEAVES_DEV, NEAR, FAR = 8, 8, 8
HALF_TILES = 14
NEAR_WEIGHT = 1.0 / 32.0
NT = ((1,), (1,))
NN = ((1,), (0,))


def split(x):
    high = x.astype(BF16)
    return high, (x - high.astype(F32)).astype(BF16)


def dot(a, b, dims):
    return lax.dot_general(a, b, (dims, ((), ())), preferred_element_type=F32)


def dot3(a, b, dims):
    return dot(a[0], b[0], dims) + (dot(a[1], b[0], dims) + dot(a[0], b[1], dims))


def kernel(
    src, pts, basis, e_hbm, f_hbm, lc_hbm, dc_hbm, gc_hbm, near_hbm, lfar_hbm, dfar_hbm, gfar_hbm,
    out,
    src_v, pts_v, basis_v, e_v, f_v, lc_v, dc_v, gc_v, dfar_v, near_s, lfar_s, gfar_s,
    w_h, w_l, rf_h, rf_l, rd_h, rd_l, rg_h, rg_l, perm_v, cols_v, acc,
    gat, table, req_v, req_s, r_out, r_in, p_out, p_in,
    loc_sem, gat_send, gat_recv, z_send, z_recv, c_sem, req_send, req_recv, req_loc, r_send, r_recv, p_send, p_recv,
):
    leaf = lax.axis_index("leaf")
    sub = lax.axis_index("sub")
    z, core = leaf // 2, lax.rem(leaf, 2)
    y, x = sub // SIDE, lax.rem(sub, SIDE)

    def at_plane(dy, dx):
        return lax.rem(y + dy, SIDE) * SIDE + lax.rem(x + dx, SIDE)

    plane = [at_plane(d // SIDE, d % SIDE) for d in range(1, NSUB)]
    others = [i + (i >= z).astype(jnp.int32) for i in range(NZ - 1)]
    mate = (leaf + 1 - 2 * core, sub)

    pairs = [
        (basis, basis_v), (e_hbm, e_v), (src, src_v), (f_hbm, f_v), (pts, pts_v), (dfar_hbm, dfar_v), (near_hbm, near_s),
        (lfar_hbm, lfar_s), (gfar_hbm, gfar_s), (dc_hbm, dc_v), (gc_hbm, gc_v), (lc_hbm, lc_v),
    ]
    loads = [pltpu.make_async_copy(a, b, loc_sem.at[i]) for i, (a, b) in enumerate(pairs)]
    for c in loads:
        c.start()
    barrier = pltpu.get_barrier_semaphore()
    for o in others:
        pl.semaphore_signal(barrier, inc=1, device_id=(o * 2 + core, sub), device_id_type=MESH)
    for o in plane:
        pl.semaphore_signal(barrier, inc=1, device_id=(leaf, o), device_id_type=MESH)
    pl.semaphore_signal(barrier, inc=1, device_id=mate, device_id_type=MESH)

    lane = lax.broadcasted_iota(jnp.int32, (1, 128), 1)
    left = lane < 64

    def keep(part, value):
        return jnp.where(left if part == 0 else jnp.logical_not(left), value, 0.0)

    def stack(value):
        return jnp.concatenate([keep(0, value), keep(1, value)], axis=0)

    def twice(value):
        return jnp.concatenate([value, value], axis=0)

    def pack(value):
        return jnp.where(left, value[0:8], value[8:16])

    def spread(value):
        turned = pltpu.roll(value, 64, 1)
        return jnp.concatenate([jnp.where(left, value, turned), jnp.where(left, turned, value)], axis=0)

    row_i = lax.broadcasted_iota(jnp.int32, (128, 128), 0)
    col_i = lax.broadcasted_iota(jnp.int32, (128, 128), 1)
    wanted = (col_i // 64) * 64 + 2 * lax.rem(col_i, 32) + lax.rem(col_i // 32, 2)
    perm_v[...] = (row_i == wanted).astype(F32).astype(BF16)

    for i in range(4):
        loads[i].wait()
    for t in range(LEAVES_DEV):
        lanes = pl.ds(t * 128, 128)
        e_pair = split(stack(e_v[pl.ds(t, 32, stride=8), :]))
        b_pair = split(twice(basis_v[t]))
        w_pair = split(dot3(e_pair, b_pair, NN))
        for k in range(2):
            w_h[pl.ds(k * 64, 64), lanes] = w_pair[0]
            w_l[pl.ds(k * 64, 64), lanes] = w_pair[1]
    signal = [jnp.concatenate([src_v[0, t], src_v[1, t]], axis=0) for t in range(LEAVES_DEV)]
    s_pair = split(jnp.concatenate(signal, axis=1))
    dev_coef = dot3(s_pair, (w_h[...], w_l[...]), NT)
    f_high, f_low = split(f_v[...])
    f_high, f_low = dot(f_high, perm_v[...], NN), dot(f_low, perm_v[...], NN)
    rf_h[...] = twice(stack(f_high)).astype(BF16)
    rf_l[...] = twice(stack(f_low)).astype(BF16)
    d_pair = split(jnp.where(left, dev_coef, 0.0) + jnp.where(left, 0.0, dev_coef))
    up = dot3(d_pair, (rf_h[...], rf_l[...]), NT)
    table[core, z, 0:8, :] = pack(dev_coef)
    table[core, z, 8:16, :] = pack(up)
    loads[4].wait()
    for t in range(LEAVES_DEV):
        slot, j = sub * 2 + t // 4, t % 4
        b_pair = split(twice(basis_v[t]))
        t_pair = (s_pair[0][:, t * 128 : t * 128 + 128], s_pair[1][:, t * 128 : t * 128 + 128])
        gat[slot, 2 * j] = src_v[0, t]
        gat[slot, 2 * j + 1] = src_v[1, t]
        gat[slot, 8 + j] = pack(dot3(t_pair, b_pair, NT))
    for half in range(2):
        gat[sub * 2 + half, 13] = jnp.zeros((8, 128), F32)
    for t in range(LEAVES_DEV):
        for i in range(3):
            gat[sub * 2 + t // 4, 12 + i // 2, pl.ds(i % 2 * 4 + t % 4, 1), :] = pts_v[i : i + 1, t * 128 : t * 128 + 128]
    loads[5].wait()
    req_v[sub] = jnp.zeros((1, 128), jnp.int32)
    req_v[sub, :, 0:8] = dfar_v[...]

    pl.semaphore_wait(barrier, 2 * NSUB - 1)

    z_copies = []
    for i, o in enumerate(others):
        z_copies.append(
            pltpu.make_async_remote_copy(
                table.at[core, z], table.at[core, z], z_send.at[i], z_recv.at[z],
                device_id=(o * 2 + core, sub), device_id_type=MESH,
            )
        )
    for c in z_copies:
        c.start()
    req_copies = []
    for i, o in enumerate(plane):
        req_copies.append(
            pltpu.make_async_remote_copy(
                req_v.at[sub], req_v.at[sub], req_send.at[i], req_recv.at[sub],
                device_id=(leaf, o), device_id_type=MESH,
            )
        )
    for c in req_copies:
        c.start()

    def half_copy(number, slot, target):
        return pltpu.make_async_remote_copy(
            gat.at[slot], gat.at[slot], gat_send.at[number], gat_recv.at[slot],
            device_id=(leaf, target), device_id_type=MESH,
        )

    steps = (1, 3, 2)
    first = []
    for half in range(2):
        for d in steps:
            target = at_plane(0, d) if half == 0 else at_plane(d, 0)
            first.append(half_copy(len(first), sub * 2 + half, target))
    for c in first:
        c.start()
    second = []

    def pass_on(half, d):
        origin = at_plane(0, d) if half == 0 else at_plane(d, 0)
        slot = origin * 2 + half
        if d:
            pltpu.make_async_remote_copy(
                gat.at[slot], gat.at[slot], gat_send.at[0], gat_recv.at[slot], device_id=(leaf, origin), device_id_type=MESH
            ).wait_recv()
        for e in steps:
            target = at_plane(e, 0) if half == 0 else at_plane(0, e)
            c = half_copy(len(first) + len(second), slot, target)
            c.start()
            second.append(c)

    for half in range(2):
        pass_on(half, 0)

    for i in range(9, 11):
        loads[i].wait()
    for given, to_h, to_l in ((dc_v, rd_h, rd_l), (gc_v, rg_h, rg_l)):
        high, low = split(given[...])
        given[...] = dot(high, perm_v[...], NN)
        for k in range(FAR):
            to_h[:, k * 128 : k * 128 + 128] = twice(stack(given[pl.ds(k, 32, stride=8), :])).astype(BF16)
        given[...] = dot(low, perm_v[...], NN)
        for k in range(FAR):
            to_l[:, k * 128 : k * 128 + 128] = twice(stack(given[pl.ds(k, 32, stride=8), :])).astype(BF16)
    fw = dot3((rf_h[0:64, :], rf_l[0:64, :]), (w_h[...], w_l[...]), NN)
    fw_pair = split(fw)
    w_h[64:128, :] = fw_pair[0]
    w_l[64:128, :] = fw_pair[1]
    for t in range(LEAVES_DEV):
        for i in range(3):
            row = pts_v[i : i + 1, t * 128 : t * 128 + 128]
            cols_v[t, i] = jnp.broadcast_to(row, (128, 128)).T

    for d in steps:
        for half in range(2):
            pass_on(half, d)

    for i, o in enumerate(plane):
        pltpu.make_async_remote_copy(
            req_v.at[o], req_v.at[o], req_send.at[i], req_recv.at[o], device_id=(leaf, o), device_id_type=MESH
        ).wait_recv()
    to_scalar = pltpu.make_async_copy(req_v, req_s, req_loc)
    to_scalar.start()

    for i, o in enumerate(others):
        pltpu.make_async_remote_copy(
            table.at[core, o], table.at[core, o], z_send.at[i], z_recv.at[o], device_id=mate, device_id_type=MESH
        ).wait_recv()
    swap = pltpu.make_async_remote_copy(
        table.at[core], table.at[core], c_sem.at[0], c_sem.at[1], device_id=mate, device_id_type=MESH
    )
    swap.start()
    to_scalar.wait()
    for i in range(6, 9):
        loads[i].wait()
    pltpu.make_async_remote_copy(
        table.at[1 - core], table.at[1 - core], c_sem.at[0], c_sem.at[1], device_id=mate, device_id_type=MESH
    ).wait_recv()

    def answer(o, k):
        number = req_s[o, 0, k]
        row = table[(number >> 4) & 1, number >> 5, 0:8, :]
        return jnp.where(jnp.full((8, 128), number & (NSUB - 1), jnp.int32) == sub, row, 0.0)

    r_copies, p_copies = [], []
    for i, o in enumerate(plane):
        for k in range(FAR):
            r_out[o, k] = answer(o, k)
        c = pltpu.make_async_remote_copy(
            r_out.at[o], r_in.at[sub], r_send.at[i], r_recv.at[sub], device_id=(leaf, o), device_id_type=MESH
        )
        c.start()
        r_copies.append(c)
    for k in range(FAR):
        r_in[sub, k] = answer(sub, k)
    pieces = []
    for k in range(FAR):
        number = gfar_s[0, k]
        pieces.append(spread(table[number & 1, number >> 1, 8:16, :]))
    part = pack(dot3(split(jnp.concatenate(pieces, axis=1)), (rg_h[...], rg_l[...]), NT))
    p_out[...] = part
    p_in[sub] = part
    for i, o in enumerate(plane):
        c = pltpu.make_async_remote_copy(
            p_out, p_in.at[sub], p_send.at[i], p_recv.at[sub], device_id=(leaf, o), device_id_type=MESH
        )
        c.start()
        p_copies.append(c)

    for half in range(2):
        for d in range(NSUB):
            dy, dx = d // SIDE, d % SIDE
            if (dy if half == 0 else dx) == 0:
                continue
            slot = at_plane(dy, dx) * 2 + half
            pltpu.make_async_remote_copy(
                gat.at[slot], gat.at[slot], gat_send.at[0], gat_recv.at[slot], device_id=(leaf, sub), device_id_type=MESH
            ).wait_recv()
    loads[11].wait()

    def one_leaf(t, carry):
        total = jnp.zeros((16, 128), F32)
        for pair in range(NEAR // 2):
            tiles, vectors = [], []
            for k in (2 * pair, 2 * pair + 1):
                number = near_s[t, k]
                slot, j = number >> 2, number & 3
                square = DELTA_SQ
                for i in range(3):
                    along = cols_v[t, i] - gat[slot, 12 + i // 2, pl.ds(i % 2 * 4 + j, 1), :]
                    square = along * along + square
                tiles.append(lax.rsqrt(square))
                vectors.append(gat[slot, pl.ds(j * 2, 2)].reshape(16, 128))
            total = total + dot3(split(jnp.concatenate(vectors, axis=1)), split(jnp.concatenate(tiles, axis=1)), NT)
        lefts, rights = [], []
        for k in range(FAR):
            number = lfar_s[t, k]
            value = gat[number >> 2, 8 + (number & 3)]
            turned = pltpu.roll(value, 64, 1)
            lefts.append(jnp.concatenate([keep(0, value), keep(0, turned), keep(1, turned), keep(1, value)], axis=0))
            rights.append(lc_v[t, pl.ds(k, 32, stride=8), :])
        local = dot3(split(jnp.concatenate(lefts, axis=1)), split(jnp.concatenate(rights, axis=1)), NT)
        l_pair = split(local)
        field = NEAR_WEIGHT * total
        for parity in range(2):
            rows = slice(parity * 16, parity * 16 + 16)
            b_pair = split(basis_v[t, pl.ds(parity, 32, stride=2), :])
            field = field + dot3((l_pair[0][rows], l_pair[1][rows]), b_pair, NN)
        acc[t] = field
        return carry

    lax.fori_loop(0, LEAVES_DEV, one_leaf, 0)

    for i, o in enumerate(plane):
        pltpu.make_async_remote_copy(
            r_in.at[o], r_in.at[o], r_send.at[i], r_recv.at[o], device_id=(leaf, o), device_id_type=MESH
        ).wait_recv()
        pltpu.make_async_remote_copy(
            p_in.at[o], p_in.at[o], p_send.at[i], p_recv.at[o], device_id=(leaf, o), device_id_type=MESH
        ).wait_recv()
    asked = r_in[0]
    grp_local = p_in[0]
    for o in range(1, NSUB):
        asked = asked + r_in[o]
        grp_local = grp_local + p_in[o]
    dev_local = dot3(split(jnp.concatenate([spread(asked[k]) for k in range(FAR)], axis=1)), (rd_h[...], rd_l[...]), NT)
    both = split(jnp.where(left, dev_local, spread(grp_local)))
    far = dot3(both, (w_h[...], w_l[...]), NN)
    for t in range(LEAVES_DEV):
        field = acc[t] + far[:, t * 128 : t * 128 + 128]
        out[0, t] = field[0:8]
        out[1, t] = field[8:16]

    for c in z_copies + req_copies + first + second + [swap] + r_copies + p_copies:
        c.wait_send()


def body(
    sources, points, basis, leaf_transfer, dev_transfer, leaf_coupling, dev_coupling, grp_coupling, near_list, leaf_far,
    dev_far, grp_far,
):
    def rows(array):
        m = array.shape[0]
        return array.reshape(m, 8, 32, 128).transpose(0, 2, 1, 3).reshape(m, 256, 128)

    any_space = pl.BlockSpec(memory_space=pl.ANY)
    vm, sm, dma = pltpu.VMEM, pltpu.SMEM, pltpu.SemaphoreType.DMA
    result = pl.pallas_call(
        kernel,
        out_shape=jax.ShapeDtypeStruct((2, 8, 8, 128), F32),
        in_specs=[any_space] * 12,
        out_specs=pl.BlockSpec(memory_space=pltpu.VMEM),
        scratch_shapes=[
            vm((2, 8, 8, 128), F32), vm((3, 1024), F32), vm((8, 64, 128), F32), vm((256, 128), F32), vm((32, 128), F32),
            vm((8, 256, 128), F32), vm((256, 128), F32), vm((256, 128), F32), vm((1, 8), jnp.int32),
            sm((8, 8), jnp.int32), sm((8, 8), jnp.int32), sm((1, 8), jnp.int32),
            vm((128, 1024), BF16), vm((128, 1024), BF16), vm((128, 128), BF16), vm((128, 128), BF16),
            vm((128, 1024), BF16), vm((128, 1024), BF16), vm((128, 1024), BF16), vm((128, 1024), BF16),
            vm((128, 128), BF16), vm((8, 3, 128, 128), F32), vm((8, 16, 128), F32),
            vm((32, HALF_TILES, 8, 128), F32), vm((2, NZ, 16, 128), F32), vm((NSUB, 1, 128), jnp.int32), sm((NSUB, 1, 128), jnp.int32),
            vm((NSUB, FAR, 8, 128), F32), vm((NSUB, FAR, 8, 128), F32), vm((8, 128), F32), vm((NSUB, 8, 128), F32),
            dma((12,)), dma((30,)), dma((32,)), dma((15,)), dma((16,)), dma((2,)), dma((15,)), dma((16,)), dma,
            dma((15,)), dma((16,)), dma((15,)), dma((16,)),
        ],
        compiler_params=pltpu.CompilerParams(collective_id=0, has_side_effects=True, vmem_limit_bytes=48 * 1024 * 1024),
    )(
        sources.reshape(2, 8, 8, 128).transpose(0, 2, 1, 3),
        points,
        basis,
        rows(leaf_transfer[None])[0],
        dev_transfer.reshape(32, 128),
        rows(leaf_coupling),
        rows(dev_coupling)[0],
        rows(grp_coupling)[0],
        near_list, leaf_far, dev_far, grp_far,
    )
    return result.transpose(0, 2, 1, 3).reshape(16, 1024)


def solution(mesh):
    both = ("leaf", "sub")
    placed = (
        P(None, both), P(None, both), P(both, None, None), P(both, None), P(both, None), P(both, None, None),
        P(both, None, None), P("leaf", None, None), P(both, None), P(both, None), P(both, None), P("leaf", None),
    )
    return jax.shard_map(body, mesh=mesh, in_specs=placed, out_specs=P(None, both), check_vma=False)
```

```python
import jax
import jax.numpy as jnp
from jax import lax
from jax.experimental import pallas as pl
from jax.experimental.pallas import tpu as pltpu
from jax.sharding import PartitionSpec as P

MESH = pl.DeviceIdType.MESH
F32, BF16 = jnp.float32, jnp.bfloat16
DELTA_SQ = 0.01
NZ, NSUB, SIDE = 16, 16, 4
LEAVES_DEV, NEAR, FAR = 8, 8, 8
HALF_TILES = 14
NEAR_WEIGHT = 1.0 / 32.0
NT = ((1,), (1,))
NN = ((1,), (0,))


def split(x):
    high = x.astype(BF16)
    return high, (x - high.astype(F32)).astype(BF16)


def dot(a, b, dims):
    return lax.dot_general(a, b, (dims, ((), ())), preferred_element_type=F32)


def dot3(a, b, dims):
    return dot(a[0], b[0], dims) + (dot(a[1], b[0], dims) + dot(a[0], b[1], dims))


def kernel(
    src, pts, basis, e_hbm, f_hbm, lc_hbm, dc_hbm, gc_hbm, near_hbm, lfar_hbm, dfar_hbm, gfar_hbm,
    out,
    src_v, pts_v, basis_v, e_v, f_v, lc_v, dc_v, gc_v, dfar_v, near_s, lfar_s, gfar_s,
    w_h, w_l, rf_h, rf_l, rd_h, rd_l, rg_h, rg_l, perm_v, cols_v, acc,
    gat, table, req_v, req_s, r_out, r_in, p_out, p_in,
    loc_sem, gat_send, gat_recv, z_send, z_recv, c_sem, req_send, req_recv, req_loc, r_send, r_recv, p_send, p_recv,
):
    leaf = lax.axis_index("leaf")
    sub = lax.axis_index("sub")
    z, core = leaf // 2, lax.rem(leaf, 2)
    y, x = sub // SIDE, lax.rem(sub, SIDE)

    def at_plane(dy, dx):
        return lax.rem(y + dy, SIDE) * SIDE + lax.rem(x + dx, SIDE)

    plane = [at_plane(d // SIDE, d % SIDE) for d in range(1, NSUB)]
    mate = (leaf + 1 - 2 * core, sub)

    pairs = [
        (basis, basis_v), (e_hbm, e_v), (src, src_v), (f_hbm, f_v), (pts, pts_v), (dfar_hbm, dfar_v), (near_hbm, near_s),
        (lfar_hbm, lfar_s), (gfar_hbm, gfar_s), (dc_hbm, dc_v), (gc_hbm, gc_v), (lc_hbm, lc_v),
    ]
    loads = [pltpu.make_async_copy(a, b, loc_sem.at[i]) for i, (a, b) in enumerate(pairs)]
    for c in loads:
        c.start()
    barrier = pltpu.get_barrier_semaphore()

    def announce(o, carry):
        pl.semaphore_signal(barrier, inc=1, device_id=(o * 2 + core, sub), device_id_type=MESH)
        return carry

    lax.fori_loop(z + 1, NZ, announce, 0)
    for o in plane:
        pl.semaphore_signal(barrier, inc=1, device_id=(leaf, o), device_id_type=MESH)
    pl.semaphore_signal(barrier, inc=1, device_id=mate, device_id_type=MESH)

    lane = lax.broadcasted_iota(jnp.int32, (1, 128), 1)
    left = lane < 64

    def keep(part, value):
        return jnp.where(left if part == 0 else jnp.logical_not(left), value, 0.0)

    def stack(value):
        return jnp.concatenate([keep(0, value), keep(1, value)], axis=0)

    def twice(value):
        return jnp.concatenate([value, value], axis=0)

    def pack(value):
        return jnp.where(left, value[0:8], value[8:16])

    def spread(value):
        turned = pltpu.roll(value, 64, 1)
        return jnp.concatenate([jnp.where(left, value, turned), jnp.where(left, turned, value)], axis=0)

    row_i = lax.broadcasted_iota(jnp.int32, (128, 128), 0)
    col_i = lax.broadcasted_iota(jnp.int32, (128, 128), 1)
    wanted = (col_i // 64) * 64 + 2 * lax.rem(col_i, 32) + lax.rem(col_i // 32, 2)
    perm_v[...] = (row_i == wanted).astype(F32).astype(BF16)

    for i in range(4):
        loads[i].wait()
    for t in range(LEAVES_DEV):
        lanes = pl.ds(t * 128, 128)
        e_pair = split(stack(e_v[pl.ds(t, 32, stride=8), :]))
        b_pair = split(twice(basis_v[t]))
        w_pair = split(dot3(e_pair, b_pair, NN))
        for k in range(2):
            w_h[pl.ds(k * 64, 64), lanes] = w_pair[0]
            w_l[pl.ds(k * 64, 64), lanes] = w_pair[1]
    signal = [jnp.concatenate([src_v[0, t], src_v[1, t]], axis=0) for t in range(LEAVES_DEV)]
    s_pair = split(jnp.concatenate(signal, axis=1))
    dev_coef = dot3(s_pair, (w_h[...], w_l[...]), NT)
    f_high, f_low = split(f_v[...])
    f_high, f_low = dot(f_high, perm_v[...], NN), dot(f_low, perm_v[...], NN)
    rf_h[...] = twice(stack(f_high)).astype(BF16)
    rf_l[...] = twice(stack(f_low)).astype(BF16)
    d_pair = split(jnp.where(left, dev_coef, 0.0) + jnp.where(left, 0.0, dev_coef))
    up = dot3(d_pair, (rf_h[...], rf_l[...]), NT)
    table[core, z, 0:8, :] = pack(dev_coef)
    table[core, z, 8:16, :] = pack(up)
    pl.semaphore_wait(barrier, NSUB + z)

    def z_copy(source, target):
        return pltpu.make_async_remote_copy(
            table.at[core, source], table.at[core, source], z_send.at[target], z_recv.at[source],
            device_id=(target * 2 + core, sub), device_id_type=MESH,
        )

    def to_lower(o, carry):
        z_copy(z, o).start()
        return carry

    lax.fori_loop(0, z, to_lower, 0)
    loads[4].wait()
    for t in range(LEAVES_DEV):
        slot, j = sub * 2 + t // 4, t % 4
        b_pair = split(twice(basis_v[t]))
        t_pair = (s_pair[0][:, t * 128 : t * 128 + 128], s_pair[1][:, t * 128 : t * 128 + 128])
        gat[slot, 2 * j] = src_v[0, t]
        gat[slot, 2 * j + 1] = src_v[1, t]
        gat[slot, 8 + j] = pack(dot3(t_pair, b_pair, NT))
    for half in range(2):
        gat[sub * 2 + half, 13] = jnp.zeros((8, 128), F32)
    for t in range(LEAVES_DEV):
        for i in range(3):
            gat[sub * 2 + t // 4, 12 + i // 2, pl.ds(i % 2 * 4 + t % 4, 1), :] = pts_v[i : i + 1, t * 128 : t * 128 + 128]
    loads[5].wait()
    req_v[sub] = jnp.zeros((1, 128), jnp.int32)
    req_v[sub, :, 0:8] = dfar_v[...]

    req_copies = []
    for i, o in enumerate(plane):
        req_copies.append(
            pltpu.make_async_remote_copy(
                req_v.at[sub], req_v.at[sub], req_send.at[i], req_recv.at[sub],
                device_id=(leaf, o), device_id_type=MESH,
            )
        )
    for c in req_copies:
        c.start()

    def half_copy(number, slot, target):
        return pltpu.make_async_remote_copy(
            gat.at[slot], gat.at[slot], gat_send.at[number], gat_recv.at[slot],
            device_id=(leaf, target), device_id_type=MESH,
        )

    steps = (1, 3, 2)
    first = []
    for half in range(2):
        for d in steps:
            target = at_plane(0, d) if half == 0 else at_plane(d, 0)
            first.append(half_copy(len(first), sub * 2 + half, target))
    for c in first:
        c.start()
    second = []

    def pass_on(half, d):
        origin = at_plane(0, d) if half == 0 else at_plane(d, 0)
        slot = origin * 2 + half
        if d:
            pltpu.make_async_remote_copy(
                gat.at[slot], gat.at[slot], gat_send.at[0], gat_recv.at[slot], device_id=(leaf, origin), device_id_type=MESH
            ).wait_recv()
        for e in steps:
            target = at_plane(e, 0) if half == 0 else at_plane(0, e)
            c = half_copy(len(first) + len(second), slot, target)
            c.start()
            second.append(c)

    for half in range(2):
        pass_on(half, 0)

    for i in range(9, 11):
        loads[i].wait()
    for given, to_h, to_l in ((dc_v, rd_h, rd_l), (gc_v, rg_h, rg_l)):
        high, low = split(given[...])
        given[...] = dot(high, perm_v[...], NN)
        for k in range(FAR):
            to_h[:, k * 128 : k * 128 + 128] = twice(stack(given[pl.ds(k, 32, stride=8), :])).astype(BF16)
        given[...] = dot(low, perm_v[...], NN)
        for k in range(FAR):
            to_l[:, k * 128 : k * 128 + 128] = twice(stack(given[pl.ds(k, 32, stride=8), :])).astype(BF16)
    fw = dot3((rf_h[0:64, :], rf_l[0:64, :]), (w_h[...], w_l[...]), NN)
    fw_pair = split(fw)
    w_h[64:128, :] = fw_pair[0]
    w_l[64:128, :] = fw_pair[1]
    for t in range(LEAVES_DEV):
        for i in range(3):
            row = pts_v[i : i + 1, t * 128 : t * 128 + 128]
            cols_v[t, i] = jnp.broadcast_to(row, (128, 128)).T

    for d in steps:
        for half in range(2):
            pass_on(half, d)

    for i, o in enumerate(plane):
        pltpu.make_async_remote_copy(
            req_v.at[o], req_v.at[o], req_send.at[i], req_recv.at[o], device_id=(leaf, o), device_id_type=MESH
        ).wait_recv()
    to_scalar = pltpu.make_async_copy(req_v, req_s, req_loc)
    to_scalar.start()

    def from_higher(o, carry):
        z_copy(o, o).wait_recv()
        z_copy(z, o).start()
        return carry

    def from_lower(o, carry):
        z_copy(o, o).wait_recv()
        return carry

    lax.fori_loop(z + 1, NZ, from_higher, 0)
    lax.fori_loop(0, z, from_lower, 0)
    swap = pltpu.make_async_remote_copy(
        table.at[core], table.at[core], c_sem.at[0], c_sem.at[1], device_id=mate, device_id_type=MESH
    )
    swap.start()
    to_scalar.wait()
    for i in range(6, 9):
        loads[i].wait()
    pltpu.make_async_remote_copy(
        table.at[1 - core], table.at[1 - core], c_sem.at[0], c_sem.at[1], device_id=mate, device_id_type=MESH
    ).wait_recv()

    def answer(o, k):
        number = req_s[o, 0, k]
        row = table[(number >> 4) & 1, number >> 5, 0:8, :]
        return jnp.where(jnp.full((8, 128), number & (NSUB - 1), jnp.int32) == sub, row, 0.0)

    r_copies, p_copies = [], []
    for i, o in enumerate(plane):
        for k in range(FAR):
            r_out[o, k] = answer(o, k)
        c = pltpu.make_async_remote_copy(
            r_out.at[o], r_in.at[sub], r_send.at[i], r_recv.at[sub], device_id=(leaf, o), device_id_type=MESH
        )
        c.start()
        r_copies.append(c)
    for k in range(FAR):
        r_in[sub, k] = answer(sub, k)
    pieces = []
    for k in range(FAR):
        number = gfar_s[0, k]
        pieces.append(spread(table[number & 1, number >> 1, 8:16, :]))
    part = pack(dot3(split(jnp.concatenate(pieces, axis=1)), (rg_h[...], rg_l[...]), NT))
    p_out[...] = part
    p_in[sub] = part
    for i, o in enumerate(plane):
        c = pltpu.make_async_remote_copy(
            p_out, p_in.at[sub], p_send.at[i], p_recv.at[sub], device_id=(leaf, o), device_id_type=MESH
        )
        c.start()
        p_copies.append(c)

    for half in range(2):
        for d in range(NSUB):
            dy, dx = d // SIDE, d % SIDE
            if (dy if half == 0 else dx) == 0:
                continue
            slot = at_plane(dy, dx) * 2 + half
            pltpu.make_async_remote_copy(
                gat.at[slot], gat.at[slot], gat_send.at[0], gat_recv.at[slot], device_id=(leaf, sub), device_id_type=MESH
            ).wait_recv()
    loads[11].wait()

    def one_leaf(t, carry):
        total = jnp.zeros((16, 128), F32)
        for pair in range(NEAR // 2):
            tiles, vectors = [], []
            for k in (2 * pair, 2 * pair + 1):
                number = near_s[t, k]
                slot, j = number >> 2, number & 3
                square = DELTA_SQ
                for i in range(3):
                    along = cols_v[t, i] - gat[slot, 12 + i // 2, pl.ds(i % 2 * 4 + j, 1), :]
                    square = along * along + square
                tiles.append(lax.rsqrt(square))
                vectors.append(gat[slot, pl.ds(j * 2, 2)].reshape(16, 128))
            total = total + dot3(split(jnp.concatenate(vectors, axis=1)), split(jnp.concatenate(tiles, axis=1)), NT)
        lefts, rights = [], []
        for k in range(FAR):
            number = lfar_s[t, k]
            value = gat[number >> 2, 8 + (number & 3)]
            turned = pltpu.roll(value, 64, 1)
            lefts.append(jnp.concatenate([keep(0, value), keep(0, turned), keep(1, turned), keep(1, value)], axis=0))
            rights.append(lc_v[t, pl.ds(k, 32, stride=8), :])
        local = dot3(split(jnp.concatenate(lefts, axis=1)), split(jnp.concatenate(rights, axis=1)), NT)
        l_pair = split(local)
        field = NEAR_WEIGHT * total
        for parity in range(2):
            rows = slice(parity * 16, parity * 16 + 16)
            b_pair = split(basis_v[t, pl.ds(parity, 32, stride=2), :])
            field = field + dot3((l_pair[0][rows], l_pair[1][rows]), b_pair, NN)
        acc[t] = field
        return carry

    lax.fori_loop(0, LEAVES_DEV, one_leaf, 0)

    for i, o in enumerate(plane):
        pltpu.make_async_remote_copy(
            r_in.at[o], r_in.at[o], r_send.at[i], r_recv.at[o], device_id=(leaf, o), device_id_type=MESH
        ).wait_recv()
        pltpu.make_async_remote_copy(
            p_in.at[o], p_in.at[o], p_send.at[i], p_recv.at[o], device_id=(leaf, o), device_id_type=MESH
        ).wait_recv()
    asked = r_in[0]
    grp_local = p_in[0]
    for o in range(1, NSUB):
        asked = asked + r_in[o]
        grp_local = grp_local + p_in[o]
    dev_local = dot3(split(jnp.concatenate([spread(asked[k]) for k in range(FAR)], axis=1)), (rd_h[...], rd_l[...]), NT)
    both = split(jnp.where(left, dev_local, spread(grp_local)))
    far = dot3(both, (w_h[...], w_l[...]), NN)
    for t in range(LEAVES_DEV):
        field = acc[t] + far[:, t * 128 : t * 128 + 128]
        out[0, t] = field[0:8]
        out[1, t] = field[8:16]

    def sent(o, carry):
        z_copy(z, o).wait_send()
        return carry

    lax.fori_loop(0, z, sent, 0)
    lax.fori_loop(z + 1, NZ, sent, 0)
    for c in req_copies + first + second + [swap] + r_copies + p_copies:
        c.wait_send()


def body(
    sources, points, basis, leaf_transfer, dev_transfer, leaf_coupling, dev_coupling, grp_coupling, near_list, leaf_far,
    dev_far, grp_far,
):
    def rows(array):
        m = array.shape[0]
        return array.reshape(m, 8, 32, 128).transpose(0, 2, 1, 3).reshape(m, 256, 128)

    in_hbm = pl.BlockSpec(memory_space=pltpu.HBM)
    vm, sm, dma = pltpu.VMEM, pltpu.SMEM, pltpu.SemaphoreType.DMA
    result = pl.pallas_call(
        kernel,
        out_shape=jax.ShapeDtypeStruct((2, 8, 8, 128), F32),
        in_specs=[in_hbm] * 12,
        out_specs=pl.BlockSpec(memory_space=pltpu.VMEM),
        scratch_shapes=[
            vm((2, 8, 8, 128), F32), vm((3, 1024), F32), vm((8, 64, 128), F32), vm((256, 128), F32), vm((32, 128), F32),
            vm((8, 256, 128), F32), vm((256, 128), F32), vm((256, 128), F32), vm((1, 8), jnp.int32),
            sm((8, 8), jnp.int32), sm((8, 8), jnp.int32), sm((1, 8), jnp.int32),
            vm((128, 1024), BF16), vm((128, 1024), BF16), vm((128, 128), BF16), vm((128, 128), BF16),
            vm((128, 1024), BF16), vm((128, 1024), BF16), vm((128, 1024), BF16), vm((128, 1024), BF16),
            vm((128, 128), BF16), vm((8, 3, 128, 128), F32), vm((8, 16, 128), F32),
            vm((32, HALF_TILES, 8, 128), F32), vm((2, NZ, 16, 128), F32), vm((NSUB, 1, 128), jnp.int32), sm((NSUB, 1, 128), jnp.int32),
            vm((NSUB, FAR, 8, 128), F32), vm((NSUB, FAR, 8, 128), F32), vm((8, 128), F32), vm((NSUB, 8, 128), F32),
            dma((12,)), dma((30,)), dma((32,)), dma((16,)), dma((16,)), dma((2,)), dma((15,)), dma((16,)), dma,
            dma((15,)), dma((16,)), dma((15,)), dma((16,)),
        ],
        compiler_params=pltpu.CompilerParams(collective_id=0, has_side_effects=True, vmem_limit_bytes=60 * 1024 * 1024),
    )(
        sources.reshape(2, 8, 8, 128).transpose(0, 2, 1, 3),
        points,
        basis,
        rows(leaf_transfer[None])[0],
        dev_transfer.reshape(32, 128),
        rows(leaf_coupling),
        rows(dev_coupling)[0],
        rows(grp_coupling)[0],
        near_list, leaf_far, dev_far, grp_far,
    )
    return result.transpose(0, 2, 1, 3).reshape(16, 1024)


def solution(mesh):
    both = ("leaf", "sub")
    placed = (
        P(None, both), P(None, both), P(both, None, None), P(both, None), P(both, None), P(both, None, None),
        P(both, None, None), P("leaf", None, None), P(both, None), P(both, None), P(both, None), P("leaf", None),
    )
    return jax.shard_map(body, mesh=mesh, in_specs=placed, out_specs=P(None, both), check_vma=False)
```

```python
import jax
import jax.numpy as jnp
from jax import lax
from jax.experimental import pallas as pl
from jax.experimental.pallas import tpu as pltpu
from jax.sharding import PartitionSpec as P

MESH = pl.DeviceIdType.MESH
F32, BF16 = jnp.float32, jnp.bfloat16
DELTA_SQ = 0.01
NZ, NSUB, SIDE = 16, 16, 4
EARLY, FAR_Z = 4, 5
LEAVES_DEV, NEAR, FAR = 8, 8, 8
HALF_TILES = 14
NEAR_WEIGHT = 1.0 / 32.0
NT = ((1,), (1,))
NN = ((1,), (0,))


def split(x):
    high = x.astype(BF16)
    return high, (x - high.astype(F32)).astype(BF16)


def dot(a, b, dims):
    return lax.dot_general(a, b, (dims, ((), ())), preferred_element_type=F32)


def dot3(a, b, dims):
    return dot(a[0], b[0], dims) + (dot(a[1], b[0], dims) + dot(a[0], b[1], dims))


def kernel(
    src, pts, basis, e_hbm, f_hbm, lc_hbm, dc_hbm, gc_hbm, near_hbm, lfar_hbm, dfar_hbm, gfar_hbm,
    out,
    src_v, pts_v, basis_v, e_v, f_v, lc_v, dc_v, gc_v, dfar_v, near_s, lfar_s, gfar_s,
    w_h, w_l, rf_h, rf_l, rd_h, rd_l, rg_h, rg_l, perm_v, cols_v, acc,
    gat, table, req_v, req_s, r_out, r_in, p_out, p_in,
    loc_sem, here_sem, gat_send, gat_recv, z_send, z_recv, c_sem, req_send, req_recv, req_loc, r_send, r_recv, p_send, p_recv,
):
    leaf = lax.axis_index("leaf")
    sub = lax.axis_index("sub")
    z, core = leaf // 2, lax.rem(leaf, 2)
    y, x = sub // SIDE, lax.rem(sub, SIDE)

    def at_plane(dy, dx):
        return lax.rem(y + dy, SIDE) * SIDE + lax.rem(x + dx, SIDE)

    ring = (0, 1, 2, 1)
    order = sorted(range(1, NSUB), key=lambda d: -ring[d // SIDE] - ring[d % SIDE])
    plane = [at_plane(d // SIDE, d % SIDE) for d in order]
    up_from = jnp.where(z < EARLY, z + 1, z + FAR_Z)
    low_end = jnp.minimum(z, EARLY)
    peer_from = jnp.maximum(EARLY, z - FAR_Z + 1)
    peer_next = jnp.where(z < EARLY, NZ, z + 1)
    peer_end = jnp.minimum(NZ, z + FAR_Z)
    late = (z >= EARLY).astype(jnp.int32)

    peers = late * (z - peer_from + peer_end - 1 - z)

    mate = (leaf + 1 - 2 * core, sub)

    barrier = pltpu.get_barrier_semaphore()
    for o in plane:
        pl.semaphore_signal(barrier, inc=1, device_id=(leaf, o), device_id_type=MESH)
    pl.semaphore_signal(barrier, inc=1, device_id=mate, device_id_type=MESH)

    def announce(o, carry):
        pl.semaphore_signal(barrier, inc=1, device_id=(o * 2 + core, sub), device_id_type=MESH)
        return carry

    lax.fori_loop(peer_from, z, announce, 0)
    lax.fori_loop(peer_next, peer_end, announce, 0)
    lax.fori_loop(up_from, NZ, announce, 0)

    pairs = [
        (basis, basis_v), (e_hbm, e_v), (src, src_v), (f_hbm, f_v), (pts, pts_v), (dfar_hbm, dfar_v), (near_hbm, near_s),
        (lfar_hbm, lfar_s), (gfar_hbm, gfar_s), (dc_hbm, dc_v), (gc_hbm, gc_v), (lc_hbm, lc_v),
    ]
    loads = [pltpu.make_async_copy(a, b, loc_sem.at[i]) for i, (a, b) in enumerate(pairs)]
    for c in loads:
        c.start()
    lane = lax.broadcasted_iota(jnp.int32, (1, 128), 1)
    left = lane < 64

    def keep(part, value):
        return jnp.where(left if part == 0 else jnp.logical_not(left), value, 0.0)

    def stack(value):
        return jnp.concatenate([keep(0, value), keep(1, value)], axis=0)

    def twice(value):
        return jnp.concatenate([value, value], axis=0)

    def pack(value):
        return jnp.where(left, value[0:8], value[8:16])

    def spread(value):
        turned = pltpu.roll(value, 64, 1)
        return jnp.concatenate([jnp.where(left, value, turned), jnp.where(left, turned, value)], axis=0)

    row_i = lax.broadcasted_iota(jnp.int32, (128, 128), 0)
    col_i = lax.broadcasted_iota(jnp.int32, (128, 128), 1)
    wanted = (col_i // 64) * 64 + 2 * lax.rem(col_i, 32) + lax.rem(col_i // 32, 2)
    perm_v[...] = (row_i == wanted).astype(F32).astype(BF16)

    for i in range(4):
        loads[i].wait()
    for t in range(LEAVES_DEV):
        lanes = pl.ds(t * 128, 128)
        e_pair = split(stack(e_v[pl.ds(t, 32, stride=8), :]))
        b_pair = split(twice(basis_v[t]))
        w_pair = split(dot3(e_pair, b_pair, NN))
        for k in range(2):
            w_h[pl.ds(k * 64, 64), lanes] = w_pair[0]
            w_l[pl.ds(k * 64, 64), lanes] = w_pair[1]
    signal = [jnp.concatenate([src_v[0, t], src_v[1, t]], axis=0) for t in range(LEAVES_DEV)]
    s_pair = split(jnp.concatenate(signal, axis=1))
    dev_coef = dot3(s_pair, (w_h[...], w_l[...]), NT)
    f_high, f_low = split(f_v[...])
    f_high, f_low = dot(f_high, perm_v[...], NN), dot(f_low, perm_v[...], NN)
    rf_h[...] = twice(stack(f_high)).astype(BF16)
    rf_l[...] = twice(stack(f_low)).astype(BF16)
    d_pair = split(jnp.where(left, dev_coef, 0.0) + jnp.where(left, 0.0, dev_coef))
    up = dot3(d_pair, (rf_h[...], rf_l[...]), NT)
    table[core, z, 0:8, :] = pack(dev_coef)
    table[core, z, 8:16, :] = pack(up)
    loads[4].wait()
    for t in range(LEAVES_DEV):
        slot, j = sub * 2 + t // 4, t % 4
        b_pair = split(twice(basis_v[t]))
        t_pair = (s_pair[0][:, t * 128 : t * 128 + 128], s_pair[1][:, t * 128 : t * 128 + 128])
        gat[slot, 2 * j] = src_v[0, t]
        gat[slot, 2 * j + 1] = src_v[1, t]
        gat[slot, 8 + j] = pack(dot3(t_pair, b_pair, NT))
    for half in range(2):
        gat[sub * 2 + half, 13] = jnp.zeros((8, 128), F32)
    for t in range(LEAVES_DEV):
        for i in range(3):
            gat[sub * 2 + t // 4, 12 + i // 2, pl.ds(i % 2 * 4 + t % 4, 1), :] = pts_v[i : i + 1, t * 128 : t * 128 + 128]
    loads[5].wait()
    req_v[sub] = jnp.zeros((1, 128), jnp.int32)
    req_v[sub, :, 0:8] = dfar_v[...]

    pl.semaphore_wait(barrier, NSUB + low_end + late * jnp.maximum(0, z - FAR_Z - EARLY + 1) + peers)

    def z_copy(source, target):
        return pltpu.make_async_remote_copy(
            table.at[core, source], table.at[core, source], z_send.at[target], z_recv.at[source],
            device_id=(target * 2 + core, sub), device_id_type=MESH,
        )

    def send_z(o, carry):
        z_copy(z, o).start()
        return carry

    def send_down(o, carry):
        pl.semaphore_signal(here_sem.at[z], inc=1, device_id=(o * 2 + core, sub), device_id_type=MESH)
        return send_z(o, carry)

    lax.fori_loop(0, low_end, send_down, 0)
    lax.fori_loop(EARLY, z - FAR_Z + 1, send_down, 0)
    lax.fori_loop(peer_from, z, send_z, 0)
    lax.fori_loop(peer_next, peer_end, send_z, 0)

    def half_copy(number, slot, target):
        return pltpu.make_async_remote_copy(
            gat.at[slot], gat.at[slot], gat_send.at[number], gat_recv.at[slot],
            device_id=(leaf, target), device_id_type=MESH,
        )

    sends = []

    def pass_on(half, d, steps):
        if d is None:
            slot, targets = sub * 2 + half, [at_plane(0, e) if half == 0 else at_plane(e, 0) for e in steps]
        else:
            origin = at_plane(0, d) if half == 0 else at_plane(d, 0)
            slot, targets = origin * 2 + half, [at_plane(e, 0) if half == 0 else at_plane(0, e) for e in steps]
            if d:
                half_copy(0, slot, origin).wait_recv()
        for target in targets:
            c = half_copy(len(sends), slot, target)
            c.start()
            sends.append(c)

    for d in (None, 0):
        for half in range(2):
            pass_on(half, d, (1, 3, 2))
    req_copies = []
    for i, o in enumerate(plane):
        req_copies.append(
            pltpu.make_async_remote_copy(
                req_v.at[sub], req_v.at[sub], req_send.at[i], req_recv.at[sub],
                device_id=(leaf, o), device_id_type=MESH,
            )
        )
    for c in req_copies:
        c.start()

    for i in range(9, 11):
        loads[i].wait()
    for given, to_h, to_l in ((dc_v, rd_h, rd_l), (gc_v, rg_h, rg_l)):
        high, low = split(given[...])
        given[...] = dot(high, perm_v[...], NN)
        for k in range(FAR):
            to_h[:, k * 128 : k * 128 + 128] = twice(stack(given[pl.ds(k, 32, stride=8), :])).astype(BF16)
        given[...] = dot(low, perm_v[...], NN)
        for k in range(FAR):
            to_l[:, k * 128 : k * 128 + 128] = twice(stack(given[pl.ds(k, 32, stride=8), :])).astype(BF16)
    for d in (1, 3):
        for half in range(2):
            pass_on(half, d, (1, 3, 2))
    fw = dot3((rf_h[0:64, :], rf_l[0:64, :]), (w_h[...], w_l[...]), NN)
    fw_pair = split(fw)
    w_h[64:128, :] = fw_pair[0]
    w_l[64:128, :] = fw_pair[1]
    for t in range(LEAVES_DEV):
        for i in range(3):
            row = pts_v[i : i + 1, t * 128 : t * 128 + 128]
            cols_v[t, i] = jnp.broadcast_to(row, (128, 128)).T

    for half in range(2):
        pass_on(half, 2, (1, 3, 2))

    for i, o in enumerate(plane):
        pltpu.make_async_remote_copy(
            req_v.at[o], req_v.at[o], req_send.at[i], req_recv.at[o], device_id=(leaf, o), device_id_type=MESH
        ).wait_recv()
    to_scalar = pltpu.make_async_copy(req_v, req_s, req_loc)
    to_scalar.start()

    def send_up(o, carry):
        pl.semaphore_wait(here_sem.at[o], 1)
        return send_z(o, carry)

    def received(o, carry):
        z_copy(o, o).wait_recv()
        return carry

    lax.fori_loop(up_from, NZ, send_up, 0)
    lax.fori_loop(up_from, NZ, received, 0)
    lax.fori_loop(peer_from, z, received, 0)
    lax.fori_loop(peer_next, peer_end, received, 0)
    lax.fori_loop(0, low_end, received, 0)
    lax.fori_loop(EARLY, z - FAR_Z + 1, received, 0)
    swap = pltpu.make_async_remote_copy(
        table.at[core], table.at[core], c_sem.at[0], c_sem.at[1], device_id=mate, device_id_type=MESH
    )
    swap.start()
    to_scalar.wait()
    for i in range(6, 9):
        loads[i].wait()
    pltpu.make_async_remote_copy(
        table.at[1 - core], table.at[1 - core], c_sem.at[0], c_sem.at[1], device_id=mate, device_id_type=MESH
    ).wait_recv()

    def answer(o, k):
        number = req_s[o, 0, k]
        row = table[(number >> 4) & 1, number >> 5, 0:8, :]
        return jnp.where(jnp.full((8, 128), number & (NSUB - 1), jnp.int32) == sub, row, 0.0)

    r_copies, p_copies = [], []
    for i, o in enumerate(plane):
        for k in range(FAR):
            r_out[o, k] = answer(o, k)
        c = pltpu.make_async_remote_copy(
            r_out.at[o], r_in.at[sub], r_send.at[i], r_recv.at[sub], device_id=(leaf, o), device_id_type=MESH
        )
        c.start()
        r_copies.append(c)
    for k in range(FAR):
        r_in[sub, k] = answer(sub, k)
    pieces = []
    for k in range(FAR):
        number = gfar_s[0, k]
        pieces.append(spread(table[number & 1, number >> 1, 8:16, :]))
    part = pack(dot3(split(jnp.concatenate(pieces, axis=1)), (rg_h[...], rg_l[...]), NT))
    p_out[...] = part
    p_in[sub] = part
    for i, o in enumerate(plane):
        c = pltpu.make_async_remote_copy(
            p_out, p_in.at[sub], p_send.at[i], p_recv.at[sub], device_id=(leaf, o), device_id_type=MESH
        )
        c.start()
        p_copies.append(c)

    for half in range(2):
        for d in range(NSUB):
            dy, dx = d // SIDE, d % SIDE
            if (dy if half == 0 else dx) == 0:
                continue
            slot = at_plane(dy, dx) * 2 + half
            pltpu.make_async_remote_copy(
                gat.at[slot], gat.at[slot], gat_send.at[0], gat_recv.at[slot], device_id=(leaf, sub), device_id_type=MESH
            ).wait_recv()
    loads[11].wait()

    def one_leaf(t, carry):
        total = jnp.zeros((16, 128), F32)
        for pair in range(NEAR // 2):
            tiles, vectors = [], []
            for k in (2 * pair, 2 * pair + 1):
                number = near_s[t, k]
                slot, j = number >> 2, number & 3
                square = DELTA_SQ
                for i in range(3):
                    along = cols_v[t, i] - gat[slot, 12 + i // 2, pl.ds(i % 2 * 4 + j, 1), :]
                    square = along * along + square
                tiles.append(lax.rsqrt(square))
                vectors.append(gat[slot, pl.ds(j * 2, 2)].reshape(16, 128))
            total = total + dot3(split(jnp.concatenate(vectors, axis=1)), split(jnp.concatenate(tiles, axis=1)), NT)
        lefts, rights = [], []
        for k in range(FAR):
            number = lfar_s[t, k]
            value = gat[number >> 2, 8 + (number & 3)]
            turned = pltpu.roll(value, 64, 1)
            lefts.append(jnp.concatenate([keep(0, value), keep(0, turned), keep(1, turned), keep(1, value)], axis=0))
            rights.append(lc_v[t, pl.ds(k, 32, stride=8), :])
        local = dot3(split(jnp.concatenate(lefts, axis=1)), split(jnp.concatenate(rights, axis=1)), NT)
        l_pair = split(local)
        field = NEAR_WEIGHT * total
        for parity in range(2):
            rows = slice(parity * 16, parity * 16 + 16)
            b_pair = split(basis_v[t, pl.ds(parity, 32, stride=2), :])
            field = field + dot3((l_pair[0][rows], l_pair[1][rows]), b_pair, NN)
        acc[t] = field
        return carry

    lax.fori_loop(0, LEAVES_DEV, one_leaf, 0)

    for i, o in enumerate(plane):
        pltpu.make_async_remote_copy(
            r_in.at[o], r_in.at[o], r_send.at[i], r_recv.at[o], device_id=(leaf, o), device_id_type=MESH
        ).wait_recv()
        pltpu.make_async_remote_copy(
            p_in.at[o], p_in.at[o], p_send.at[i], p_recv.at[o], device_id=(leaf, o), device_id_type=MESH
        ).wait_recv()
    asked = r_in[0]
    grp_local = p_in[0]
    for o in range(1, NSUB):
        asked = asked + r_in[o]
        grp_local = grp_local + p_in[o]
    dev_local = dot3(split(jnp.concatenate([spread(asked[k]) for k in range(FAR)], axis=1)), (rd_h[...], rd_l[...]), NT)
    both = split(jnp.where(left, dev_local, spread(grp_local)))
    far = dot3(both, (w_h[...], w_l[...]), NN)
    for t in range(LEAVES_DEV):
        field = acc[t] + far[:, t * 128 : t * 128 + 128]
        out[0, t] = field[0:8]
        out[1, t] = field[8:16]

    def sent(o, carry):
        z_copy(z, o).wait_send()
        return carry

    lax.fori_loop(0, z, sent, 0)
    lax.fori_loop(z + 1, NZ, sent, 0)
    for c in req_copies + sends + [swap] + r_copies + p_copies:
        c.wait_send()


def body(
    sources, points, basis, leaf_transfer, dev_transfer, leaf_coupling, dev_coupling, grp_coupling, near_list, leaf_far,
    dev_far, grp_far,
):
    def rows(array):
        m = array.shape[0]
        return array.reshape(m, 8, 32, 128).transpose(0, 2, 1, 3).reshape(m, 256, 128)

    in_hbm = pl.BlockSpec(memory_space=pltpu.HBM)
    vm, sm, dma = pltpu.VMEM, pltpu.SMEM, pltpu.SemaphoreType.DMA
    result = pl.pallas_call(
        kernel,
        out_shape=pltpu.VMEM((2, 8, 8, 128), F32),
        in_specs=[in_hbm] * 12,
        out_specs=pl.BlockSpec(memory_space=pltpu.VMEM),
        scratch_shapes=[
            vm((2, 8, 8, 128), F32), vm((3, 1024), F32), vm((8, 64, 128), F32), vm((256, 128), F32), vm((32, 128), F32),
            vm((8, 256, 128), F32), vm((256, 128), F32), vm((256, 128), F32), vm((1, 8), jnp.int32),
            sm((8, 8), jnp.int32), sm((8, 8), jnp.int32), sm((1, 8), jnp.int32),
            vm((128, 1024), BF16), vm((128, 1024), BF16), vm((128, 128), BF16), vm((128, 128), BF16),
            vm((128, 1024), BF16), vm((128, 1024), BF16), vm((128, 1024), BF16), vm((128, 1024), BF16),
            vm((128, 128), BF16), vm((8, 3, 128, 128), F32), vm((8, 16, 128), F32),
            vm((32, HALF_TILES, 8, 128), F32), vm((2, NZ, 16, 128), F32), vm((NSUB, 1, 128), jnp.int32), sm((NSUB, 1, 128), jnp.int32),
            vm((NSUB, FAR, 8, 128), F32), vm((NSUB, FAR, 8, 128), F32), vm((8, 128), F32), vm((NSUB, 8, 128), F32),
            dma((12,)), pltpu.SemaphoreType.REGULAR((NZ,)), dma((30,)), dma((32,)), dma((16,)), dma((16,)), dma((2,)), dma((15,)), dma((16,)), dma,
            dma((15,)), dma((16,)), dma((15,)), dma((16,)),
        ],
        compiler_params=pltpu.CompilerParams(collective_id=0, has_side_effects=True, vmem_limit_bytes=60 * 1024 * 1024),
    )(
        sources.reshape(2, 8, 8, 128).transpose(0, 2, 1, 3),
        points,
        basis,
        rows(leaf_transfer[None])[0],
        dev_transfer.reshape(32, 128),
        rows(leaf_coupling),
        rows(dev_coupling)[0],
        rows(grp_coupling)[0],
        near_list, leaf_far, dev_far, grp_far,
    )
    return result.transpose(0, 2, 1, 3).reshape(16, 1024)


def solution(mesh):
    both = ("leaf", "sub")
    placed = (
        P(None, both), P(None, both), P(both, None, None), P(both, None), P(both, None), P(both, None, None),
        P(both, None, None), P("leaf", None, None), P(both, None), P(both, None), P(both, None), P("leaf", None),
    )
    return jax.shard_map(body, mesh=mesh, in_specs=placed, out_specs=P(None, both), check_vma=False)
```

```python
import jax
import jax.numpy as jnp
from jax import lax
from jax.experimental import pallas as pl
from jax.experimental.pallas import tpu as pltpu
from jax.sharding import PartitionSpec as P

MESH = pl.DeviceIdType.MESH
F32, BF16 = jnp.float32, jnp.bfloat16
DELTA_SQ = 0.01
NZ, NSUB, SIDE = 16, 16, 4
EARLY, FAR_Z, NEAR_Z = 4, 9, 5
LEAVES_DEV, NEAR, FAR = 8, 8, 8
HALF_TILES = 14
NEAR_WEIGHT = 1.0 / 32.0
NT = ((1,), (1,))
NN = ((1,), (0,))


def split(x):
    high = x.astype(BF16)
    return high, (x - high.astype(F32)).astype(BF16)


def dot(a, b, dims):
    return lax.dot_general(a, b, (dims, ((), ())), preferred_element_type=F32)


def dot3(a, b, dims):
    m = a[0].shape[0]
    both = dot(jnp.concatenate(a, axis=0), b[0], dims)
    return both[:m] + (both[m:] + dot(a[0], b[1], dims))


def kernel(
    src, pts, basis, e_hbm, f_hbm, lc_hbm, dc_hbm, gc_hbm, near_hbm, lfar_hbm, dfar_hbm, gfar_hbm,
    out,
    src_v, pts_v, basis_v, e_v, f_v, lc_v, dc_v, gc_v, dfar_v, near_s, lfar_s, gfar_s,
    w_h, w_l, rf_h, rf_l, rd_h, rd_l, rg_h, rg_l, perm_v, cols_v, acc,
    gat, table, req_v, req_s, r_out, r_in, p_out, p_in,
    loc_sem, here_sem, step_sem, gat_send, gat_recv, z_send, z_recv, c_sem, req_send, req_recv, req_loc, r_send, r_recv, p_send, p_recv,
):
    leaf = lax.axis_index("leaf")
    sub = lax.axis_index("sub")
    z, core = leaf // 2, lax.rem(leaf, 2)
    y, x = sub // SIDE, lax.rem(sub, SIDE)

    def at_plane(dy, dx):
        return lax.rem(y + dy, SIDE) * SIDE + lax.rem(x + dx, SIDE)

    ring = (0, 1, 2, 1)
    order = sorted(range(1, NSUB), key=lambda d: -ring[d // SIDE] - ring[d % SIDE])
    plane = [at_plane(d // SIDE, d % SIDE) for d in order]
    late = (z >= EARLY).astype(jnp.int32)
    up_from = jnp.where(z < EARLY, z + 1, z + FAR_Z)
    low_end = jnp.minimum(z, EARLY)
    near_from = jnp.maximum(EARLY, z - NEAR_Z + 1)
    near_next = jnp.where(z < EARLY, NZ, z + 1)
    near_end = jnp.minimum(NZ, z + NEAR_Z)
    mid_from = jnp.maximum(EARLY, z - FAR_Z + 1)
    mid_next = jnp.where(z < EARLY, NZ, z + NEAR_Z)
    mid_end = jnp.minimum(NZ, z + FAR_Z)
    peers = late * (near_end - 1 - near_from)

    mate = (leaf + 1 - 2 * core, sub)

    barrier = pltpu.get_barrier_semaphore()
    for o in plane:
        pl.semaphore_signal(barrier, inc=1, device_id=(leaf, o), device_id_type=MESH)
    pl.semaphore_signal(barrier, inc=1, device_id=mate, device_id_type=MESH)

    def announce(o, carry):
        pl.semaphore_signal(barrier, inc=1, device_id=(o * 2 + core, sub), device_id_type=MESH)
        return carry

    lax.fori_loop(near_from, z, announce, 0)
    lax.fori_loop(near_next, near_end, announce, 0)
    lax.fori_loop(up_from, NZ, announce, 0)

    pairs = [
        (basis, basis_v), (e_hbm, e_v), (src, src_v), (f_hbm, f_v), (pts, pts_v), (dfar_hbm, dfar_v), (near_hbm, near_s),
        (lfar_hbm, lfar_s), (gfar_hbm, gfar_s), (dc_hbm, dc_v), (gc_hbm, gc_v), (lc_hbm, lc_v),
    ]
    loads = [pltpu.make_async_copy(a, b, loc_sem.at[i]) for i, (a, b) in enumerate(pairs)]
    for c in loads:
        c.start()
    lane = lax.broadcasted_iota(jnp.int32, (1, 128), 1)
    left = lane < 64

    def keep(part, value):
        return jnp.where(left if part == 0 else jnp.logical_not(left), value, 0.0)

    def stack(value):
        return jnp.concatenate([keep(0, value), keep(1, value)], axis=0)

    def twice(value):
        return jnp.concatenate([value, value], axis=0)

    def pack(value):
        return jnp.where(left, value[0:8], value[8:16])

    def spread(value):
        turned = pltpu.roll(value, 64, 1)
        return jnp.concatenate([jnp.where(left, value, turned), jnp.where(left, turned, value)], axis=0)

    row_i = lax.broadcasted_iota(jnp.int32, (128, 128), 0)
    col_i = lax.broadcasted_iota(jnp.int32, (128, 128), 1)
    wanted = (col_i // 64) * 64 + 2 * lax.rem(col_i, 32) + lax.rem(col_i // 32, 2)
    perm_v[...] = (row_i == wanted).astype(F32).astype(BF16)

    for i in range(4):
        loads[i].wait()
    for t in range(LEAVES_DEV):
        lanes = pl.ds(t * 128, 128)
        e_pair = split(stack(e_v[pl.ds(t, 32, stride=8), :]))
        b_pair = split(twice(basis_v[t]))
        w_pair = split(dot3(e_pair, b_pair, NN))
        for k in range(2):
            w_h[pl.ds(k * 64, 64), lanes] = w_pair[0]
            w_l[pl.ds(k * 64, 64), lanes] = w_pair[1]
    signal = [jnp.concatenate([src_v[0, t], src_v[1, t]], axis=0) for t in range(LEAVES_DEV)]
    s_pair = split(jnp.concatenate(signal, axis=1))
    dev_coef = dot3(s_pair, (w_h[...], w_l[...]), NT)
    f_high, f_low = split(f_v[...])
    f_high, f_low = dot(f_high, perm_v[...], NN), dot(f_low, perm_v[...], NN)
    rf_h[...] = twice(stack(f_high)).astype(BF16)
    rf_l[...] = twice(stack(f_low)).astype(BF16)
    d_pair = split(jnp.where(left, dev_coef, 0.0) + jnp.where(left, 0.0, dev_coef))
    up = dot3(d_pair, (rf_h[...], rf_l[...]), NT)
    table[core, z, 0:8, :] = pack(dev_coef)
    table[core, z, 8:16, :] = pack(up)
    loads[4].wait()
    for t in range(LEAVES_DEV):
        slot, j = sub * 2 + t // 4, t % 4
        b_pair = split(twice(basis_v[t]))
        t_pair = (s_pair[0][:, t * 128 : t * 128 + 128], s_pair[1][:, t * 128 : t * 128 + 128])
        gat[slot, 2 * j] = src_v[0, t]
        gat[slot, 2 * j + 1] = src_v[1, t]
        gat[slot, 8 + j] = pack(dot3(t_pair, b_pair, NT))
    for half in range(2):
        gat[sub * 2 + half, 13] = jnp.zeros((8, 128), F32)
    for t in range(LEAVES_DEV):
        for i in range(3):
            gat[sub * 2 + t // 4, 12 + i // 2, pl.ds(i % 2 * 4 + t % 4, 1), :] = pts_v[i : i + 1, t * 128 : t * 128 + 128]
    loads[5].wait()
    req_v[sub] = jnp.zeros((1, 128), jnp.int32)
    req_v[sub, :, 0:8] = dfar_v[...]

    pl.semaphore_wait(barrier, NSUB + low_end + late * jnp.maximum(0, z - FAR_Z - EARLY + 1) + peers)

    def z_copy(source, target):
        return pltpu.make_async_remote_copy(
            table.at[core, source], table.at[core, source], z_send.at[target], z_recv.at[source],
            device_id=(target * 2 + core, sub), device_id_type=MESH,
        )

    def send_z(o, carry):
        z_copy(z, o).start()
        return carry

    def send_down(o, carry):
        pl.semaphore_signal(here_sem.at[z], inc=1, device_id=(o * 2 + core, sub), device_id_type=MESH)
        return send_z(o, carry)

    lax.fori_loop(0, low_end, send_down, 0)
    lax.fori_loop(EARLY, z - FAR_Z + 1, send_down, 0)

    def tell(o, carry):
        pl.semaphore_signal(step_sem, inc=1, device_id=(o * 2 + core, sub), device_id_type=MESH)
        return carry

    step = NEAR_Z - 1
    lax.fori_loop(jnp.where(z - step < EARLY, NZ, z - step), z - step + 1, tell, 0)
    lax.fori_loop(jnp.where(z < EARLY, NZ, z + step), jnp.minimum(NZ, z + step + 1), tell, 0)
    lax.fori_loop(near_from, z, send_z, 0)
    lax.fori_loop(near_next, near_end, send_z, 0)

    def half_copy(number, slot, target):
        return pltpu.make_async_remote_copy(
            gat.at[slot], gat.at[slot], gat_send.at[number], gat_recv.at[slot],
            device_id=(leaf, target), device_id_type=MESH,
        )

    sends = []

    def pass_on(half, d, steps):
        if d is None:
            slot, targets = sub * 2 + half, [at_plane(0, e) if half == 0 else at_plane(e, 0) for e in steps]
        else:
            origin = at_plane(0, d) if half == 0 else at_plane(d, 0)
            slot, targets = origin * 2 + half, [at_plane(e, 0) if half == 0 else at_plane(0, e) for e in steps]
            if d:
                half_copy(0, slot, origin).wait_recv()
        for target in targets:
            c = half_copy(len(sends), slot, target)
            c.start()
            sends.append(c)

    for d in (None, 0):
        for half in range(2):
            pass_on(half, d, (1, 3, 2))
    req_copies = []
    for i, o in enumerate(plane):
        req_copies.append(
            pltpu.make_async_remote_copy(
                req_v.at[sub], req_v.at[sub], req_send.at[i], req_recv.at[sub],
                device_id=(leaf, o), device_id_type=MESH,
            )
        )
    for c in req_copies:
        c.start()

    for i in range(9, 11):
        loads[i].wait()
    for given, to_h, to_l in ((dc_v, rd_h, rd_l), (gc_v, rg_h, rg_l)):
        high, low = split(given[...])
        given[...] = dot(high, perm_v[...], NN)
        for k in range(FAR):
            to_h[:, k * 128 : k * 128 + 128] = twice(stack(given[pl.ds(k, 32, stride=8), :])).astype(BF16)
        given[...] = dot(low, perm_v[...], NN)
        for k in range(FAR):
            to_l[:, k * 128 : k * 128 + 128] = twice(stack(given[pl.ds(k, 32, stride=8), :])).astype(BF16)
    for d in (1, 3):
        for half in range(2):
            pass_on(half, d, (1, 3, 2))
    told = (z - step >= EARLY).astype(jnp.int32) + late * (z + step < NZ).astype(jnp.int32)

    @pl.when(told > 0)
    def _():
        pl.semaphore_wait(step_sem, told)

    lax.fori_loop(mid_from, z - NEAR_Z + 1, send_z, 0)
    lax.fori_loop(mid_next, mid_end, send_z, 0)
    fw = dot3((rf_h[0:64, :], rf_l[0:64, :]), (w_h[...], w_l[...]), NN)
    fw_pair = split(fw)
    w_h[64:128, :] = fw_pair[0]
    w_l[64:128, :] = fw_pair[1]
    for t in range(LEAVES_DEV):
        for i in range(3):
            row = pts_v[i : i + 1, t * 128 : t * 128 + 128]
            cols_v[t, i] = jnp.broadcast_to(row, (128, 128)).T

    for half in range(2):
        pass_on(half, 2, (1, 3, 2))

    for i, o in enumerate(plane):
        pltpu.make_async_remote_copy(
            req_v.at[o], req_v.at[o], req_send.at[i], req_recv.at[o], device_id=(leaf, o), device_id_type=MESH
        ).wait_recv()
    to_scalar = pltpu.make_async_copy(req_v, req_s, req_loc)
    to_scalar.start()

    def send_up(o, carry):
        pl.semaphore_wait(here_sem.at[o], 1)
        return send_z(o, carry)

    def received(o, carry):
        z_copy(o, o).wait_recv()
        return carry

    lax.fori_loop(up_from, NZ, send_up, 0)
    lax.fori_loop(up_from, NZ, received, 0)
    lax.fori_loop(near_from, z, received, 0)
    lax.fori_loop(near_next, near_end, received, 0)
    lax.fori_loop(mid_from, z - NEAR_Z + 1, received, 0)
    lax.fori_loop(mid_next, mid_end, received, 0)
    lax.fori_loop(0, low_end, received, 0)
    lax.fori_loop(EARLY, z - FAR_Z + 1, received, 0)
    swap = pltpu.make_async_remote_copy(
        table.at[core], table.at[core], c_sem.at[0], c_sem.at[1], device_id=mate, device_id_type=MESH
    )
    swap.start()
    to_scalar.wait()
    for i in range(6, 9):
        loads[i].wait()
    pltpu.make_async_remote_copy(
        table.at[1 - core], table.at[1 - core], c_sem.at[0], c_sem.at[1], device_id=mate, device_id_type=MESH
    ).wait_recv()

    def answer(o, k):
        number = req_s[o, 0, k]
        row = table[(number >> 4) & 1, number >> 5, 0:8, :]
        return jnp.where(jnp.full((8, 128), number & (NSUB - 1), jnp.int32) == sub, row, 0.0)

    r_copies, p_copies = [], []
    for i, o in enumerate(plane):
        for k in range(FAR):
            r_out[o, k] = answer(o, k)
        c = pltpu.make_async_remote_copy(
            r_out.at[o], r_in.at[sub], r_send.at[i], r_recv.at[sub], device_id=(leaf, o), device_id_type=MESH
        )
        c.start()
        r_copies.append(c)
    for k in range(FAR):
        r_in[sub, k] = answer(sub, k)
    pieces = []
    for k in range(FAR):
        number = gfar_s[0, k]
        pieces.append(spread(table[number & 1, number >> 1, 8:16, :]))
    part = pack(dot3(split(jnp.concatenate(pieces, axis=1)), (rg_h[...], rg_l[...]), NT))
    p_out[...] = part
    p_in[sub] = part
    for i, o in enumerate(plane):
        c = pltpu.make_async_remote_copy(
            p_out, p_in.at[sub], p_send.at[i], p_recv.at[sub], device_id=(leaf, o), device_id_type=MESH
        )
        c.start()
        p_copies.append(c)

    for half in range(2):
        for d in range(NSUB):
            dy, dx = d // SIDE, d % SIDE
            if (dy if half == 0 else dx) == 0:
                continue
            slot = at_plane(dy, dx) * 2 + half
            pltpu.make_async_remote_copy(
                gat.at[slot], gat.at[slot], gat_send.at[0], gat_recv.at[slot], device_id=(leaf, sub), device_id_type=MESH
            ).wait_recv()
    loads[11].wait()

    def one_leaf(t, carry):
        total = jnp.zeros((16, 128), F32)
        for pair in range(NEAR // 2):
            tiles, vectors = [], []
            for k in (2 * pair, 2 * pair + 1):
                number = near_s[t, k]
                slot, j = number >> 2, number & 3
                square = DELTA_SQ
                for i in range(3):
                    along = cols_v[t, i] - gat[slot, 12 + i // 2, pl.ds(i % 2 * 4 + j, 1), :]
                    square = along * along + square
                tiles.append(lax.rsqrt(square))
                vectors.append(gat[slot, pl.ds(j * 2, 2)].reshape(16, 128))
            total = total + dot3(split(jnp.concatenate(vectors, axis=1)), split(jnp.concatenate(tiles, axis=1)), NT)
        lefts, rights = [], []
        for k in range(FAR):
            number = lfar_s[t, k]
            value = gat[number >> 2, 8 + (number & 3)]
            turned = pltpu.roll(value, 64, 1)
            lefts.append(jnp.concatenate([keep(0, value), keep(0, turned), keep(1, turned), keep(1, value)], axis=0))
            rights.append(lc_v[t, pl.ds(k, 32, stride=8), :])
        local = dot3(split(jnp.concatenate(lefts, axis=1)), split(jnp.concatenate(rights, axis=1)), NT)
        l_pair = split(local)
        field = NEAR_WEIGHT * total
        for parity in range(2):
            rows = slice(parity * 16, parity * 16 + 16)
            b_pair = split(basis_v[t, pl.ds(parity, 32, stride=2), :])
            field = field + dot3((l_pair[0][rows], l_pair[1][rows]), b_pair, NN)
        acc[t] = field
        return carry

    lax.fori_loop(0, LEAVES_DEV, one_leaf, 0)

    for i, o in enumerate(plane):
        pltpu.make_async_remote_copy(
            r_in.at[o], r_in.at[o], r_send.at[i], r_recv.at[o], device_id=(leaf, o), device_id_type=MESH
        ).wait_recv()
        pltpu.make_async_remote_copy(
            p_in.at[o], p_in.at[o], p_send.at[i], p_recv.at[o], device_id=(leaf, o), device_id_type=MESH
        ).wait_recv()
    asked = r_in[0]
    grp_local = p_in[0]
    for o in range(1, NSUB):
        asked = asked + r_in[o]
        grp_local = grp_local + p_in[o]
    dev_local = dot3(split(jnp.concatenate([spread(asked[k]) for k in range(FAR)], axis=1)), (rd_h[...], rd_l[...]), NT)
    both = split(jnp.where(left, dev_local, spread(grp_local)))
    far = dot3(both, (w_h[...], w_l[...]), NN)
    for t in range(LEAVES_DEV):
        field = acc[t] + far[:, t * 128 : t * 128 + 128]
        out[0, t] = field[0:8]
        out[1, t] = field[8:16]

    def sent(o, carry):
        z_copy(z, o).wait_send()
        return carry

    lax.fori_loop(0, z, sent, 0)
    lax.fori_loop(z + 1, NZ, sent, 0)
    for c in req_copies + sends + [swap] + r_copies + p_copies:
        c.wait_send()


def body(
    sources, points, basis, leaf_transfer, dev_transfer, leaf_coupling, dev_coupling, grp_coupling, near_list, leaf_far,
    dev_far, grp_far,
):
    def rows(array):
        m = array.shape[0]
        return array.reshape(m, 8, 32, 128).transpose(0, 2, 1, 3).reshape(m, 256, 128)

    in_hbm = pl.BlockSpec(memory_space=pltpu.HBM)
    vm, sm, dma = pltpu.VMEM, pltpu.SMEM, pltpu.SemaphoreType.DMA
    result = pl.pallas_call(
        kernel,
        out_shape=pltpu.VMEM((2, 8, 8, 128), F32),
        in_specs=[in_hbm] * 12,
        out_specs=pl.BlockSpec(memory_space=pltpu.VMEM),
        scratch_shapes=[
            vm((2, 8, 8, 128), F32), vm((3, 1024), F32), vm((8, 64, 128), F32), vm((256, 128), F32), vm((32, 128), F32),
            vm((8, 256, 128), F32), vm((256, 128), F32), vm((256, 128), F32), vm((1, 8), jnp.int32),
            sm((8, 8), jnp.int32), sm((8, 8), jnp.int32), sm((1, 8), jnp.int32),
            vm((128, 1024), BF16), vm((128, 1024), BF16), vm((128, 128), BF16), vm((128, 128), BF16),
            vm((128, 1024), BF16), vm((128, 1024), BF16), vm((128, 1024), BF16), vm((128, 1024), BF16),
            vm((128, 128), BF16), vm((8, 3, 128, 128), F32), vm((8, 16, 128), F32),
            vm((32, HALF_TILES, 8, 128), F32), vm((2, NZ, 16, 128), F32), vm((NSUB, 1, 128), jnp.int32), sm((NSUB, 1, 128), jnp.int32),
            vm((NSUB, FAR, 8, 128), F32), vm((NSUB, FAR, 8, 128), F32), vm((8, 128), F32), vm((NSUB, 8, 128), F32),
            dma((12,)), pltpu.SemaphoreType.REGULAR((NZ,)), pltpu.SemaphoreType.REGULAR, dma((30,)), dma((32,)), dma((16,)), dma((16,)), dma((2,)), dma((15,)), dma((16,)), dma,
            dma((15,)), dma((16,)), dma((15,)), dma((16,)),
        ],
        compiler_params=pltpu.CompilerParams(collective_id=0, has_side_effects=True, vmem_limit_bytes=60 * 1024 * 1024),
    )(
        sources.reshape(2, 8, 8, 128).transpose(0, 2, 1, 3),
        points,
        basis,
        rows(leaf_transfer[None])[0],
        dev_transfer.reshape(32, 128),
        rows(leaf_coupling),
        rows(dev_coupling)[0],
        rows(grp_coupling)[0],
        near_list, leaf_far, dev_far, grp_far,
    )
    return result.transpose(0, 2, 1, 3).reshape(16, 1024)


def solution(mesh):
    both = ("leaf", "sub")
    placed = (
        P(None, both), P(None, both), P(both, None, None), P(both, None), P(both, None), P(both, None, None),
        P(both, None, None), P("leaf", None, None), P(both, None), P(both, None), P(both, None), P("leaf", None),
    )
    return jax.shard_map(body, mesh=mesh, in_specs=placed, out_specs=P(None, both), check_vma=False)
```

```python
import jax
import jax.numpy as jnp
from jax import lax
from jax.experimental import pallas as pl
from jax.experimental.pallas import tpu as pltpu
from jax.sharding import PartitionSpec as P

MESH = pl.DeviceIdType.MESH
F32, BF16 = jnp.float32, jnp.bfloat16
DELTA_SQ = 0.01
NZ, NSUB, SIDE = 16, 16, 4
EARLY, FAR_Z, NEAR_Z = 4, 9, 5
LEAVES_DEV, NEAR, FAR = 8, 8, 8
HALF_TILES = 14
NEAR_WEIGHT = 1.0 / 32.0
NT = ((1,), (1,))
NN = ((1,), (0,))


def split(x):
    high = x.astype(BF16)
    return high, (x - high.astype(F32)).astype(BF16)


def dot(a, b, dims):
    return lax.dot_general(a, b, (dims, ((), ())), preferred_element_type=F32)


def dot3(a, b, dims):
    m = a[0].shape[0]
    both = dot(jnp.concatenate(a, axis=0), b[0], dims)
    return both[:m] + (both[m:] + dot(a[0], b[1], dims))


def kernel(
    src, pts, basis, e_hbm, f_hbm, lc_hbm, dc_hbm, gc_hbm, near_hbm, lfar_hbm, dfar_hbm, gfar_hbm,
    out,
    src_v, pts_v, basis_v, e_v, f_v, lc_v, dc_v, gc_v, dfar_v, near_s, lfar_s, gfar_s,
    w_h, w_l, rf_h, rf_l, rd_h, rd_l, rg_h, rg_l, perm_v, cols_v, acc,
    gat, table, req_v, req_s, r_out, r_in, p_out, p_in,
    loc_sem, here_sem, step_sem, gat_send, gat_recv, z_send, z_recv, c_sem, req_send, req_recv, req_loc, r_send, r_recv, p_send, p_recv,
):
    leaf = lax.axis_index("leaf")
    sub = lax.axis_index("sub")
    z, core = leaf // 2, lax.rem(leaf, 2)
    y, x = sub // SIDE, lax.rem(sub, SIDE)

    def at_plane(dy, dx):
        return lax.rem(y + dy, SIDE) * SIDE + lax.rem(x + dx, SIDE)

    ring = (0, 1, 2, 1)
    order = sorted(range(1, NSUB), key=lambda d: -ring[d // SIDE] - ring[d % SIDE])
    plane = [at_plane(d // SIDE, d % SIDE) for d in order]
    late = (z >= EARLY).astype(jnp.int32)
    up_from = jnp.where(z < EARLY, z + 1, z + FAR_Z)
    low_end = jnp.minimum(z, EARLY)
    near_from = jnp.maximum(EARLY, z - NEAR_Z + 1)
    near_next = jnp.where(z < EARLY, NZ, z + 1)
    near_end = jnp.minimum(NZ, z + NEAR_Z)
    mid_from = jnp.maximum(EARLY, z - FAR_Z + 1)
    mid_next = jnp.where(z < EARLY, NZ, z + NEAR_Z)
    mid_end = jnp.minimum(NZ, z + FAR_Z)
    peers = late * (near_end - 1 - near_from)

    mate = (leaf + 1 - 2 * core, sub)

    barrier = pltpu.get_barrier_semaphore()
    for o in plane:
        pl.semaphore_signal(barrier, inc=1, device_id=(leaf, o), device_id_type=MESH)
    pl.semaphore_signal(barrier, inc=1, device_id=mate, device_id_type=MESH)

    def announce(o, carry):
        pl.semaphore_signal(barrier, inc=1, device_id=(o * 2 + core, sub), device_id_type=MESH)
        return carry

    lax.fori_loop(near_from, z, announce, 0)
    lax.fori_loop(near_next, near_end, announce, 0)
    lax.fori_loop(up_from, NZ, announce, 0)

    pairs = [
        (basis, basis_v), (e_hbm, e_v), (src, src_v), (f_hbm, f_v), (pts, pts_v), (dfar_hbm, dfar_v), (near_hbm, near_s),
        (lfar_hbm, lfar_s), (gfar_hbm, gfar_s), (dc_hbm, dc_v), (gc_hbm, gc_v), (lc_hbm, lc_v),
    ]
    loads = [pltpu.make_async_copy(a, b, loc_sem.at[i]) for i, (a, b) in enumerate(pairs)]
    for c in loads:
        c.start()
    lane = lax.broadcasted_iota(jnp.int32, (1, 128), 1)
    left = lane < 64

    def keep(part, value):
        return jnp.where(left if part == 0 else jnp.logical_not(left), value, 0.0)

    def stack(value):
        return jnp.concatenate([keep(0, value), keep(1, value)], axis=0)

    def twice(value):
        return jnp.concatenate([value, value], axis=0)

    def pack(value):
        return jnp.where(left, value[0:8], value[8:16])

    def spread(value):
        turned = pltpu.roll(value, 64, 1)
        return jnp.concatenate([jnp.where(left, value, turned), jnp.where(left, turned, value)], axis=0)

    row_i = lax.broadcasted_iota(jnp.int32, (128, 128), 0)
    col_i = lax.broadcasted_iota(jnp.int32, (128, 128), 1)
    wanted = (col_i // 64) * 64 + 2 * lax.rem(col_i, 32) + lax.rem(col_i // 32, 2)
    perm_v[...] = (row_i == wanted).astype(F32).astype(BF16)

    for i in range(4):
        loads[i].wait()
    for t in range(LEAVES_DEV):
        lanes = pl.ds(t * 128, 128)
        e_pair = split(stack(e_v[pl.ds(t, 32, stride=8), :]))
        b_pair = split(twice(basis_v[t]))
        w_pair = split(dot3(e_pair, b_pair, NN))
        for k in range(2):
            w_h[pl.ds(k * 64, 64), lanes] = w_pair[0]
            w_l[pl.ds(k * 64, 64), lanes] = w_pair[1]
    signal = [jnp.concatenate([src_v[0, t], src_v[1, t]], axis=0) for t in range(LEAVES_DEV)]
    s_pair = split(jnp.concatenate(signal, axis=1))
    dev_coef = dot3(s_pair, (w_h[...], w_l[...]), NT)
    f_high, f_low = split(f_v[...])
    f_high, f_low = dot(f_high, perm_v[...], NN), dot(f_low, perm_v[...], NN)
    rf_h[...] = twice(stack(f_high)).astype(BF16)
    rf_l[...] = twice(stack(f_low)).astype(BF16)
    d_pair = split(jnp.where(left, dev_coef, 0.0) + jnp.where(left, 0.0, dev_coef))
    up = dot3(d_pair, (rf_h[...], rf_l[...]), NT)
    table[core, z, 0:8, :] = pack(dev_coef)
    table[core, z, 8:16, :] = pack(up)
    loads[4].wait()
    for t in range(LEAVES_DEV):
        slot, j = sub * 2 + t // 4, t % 4
        b_pair = split(twice(basis_v[t]))
        t_pair = (s_pair[0][:, t * 128 : t * 128 + 128], s_pair[1][:, t * 128 : t * 128 + 128])
        gat[slot, 2 * j] = src_v[0, t]
        gat[slot, 2 * j + 1] = src_v[1, t]
        gat[slot, 8 + j] = pack(dot3(t_pair, b_pair, NT))
    for half in range(2):
        gat[sub * 2 + half, 13] = jnp.zeros((8, 128), F32)
    for t in range(LEAVES_DEV):
        for i in range(3):
            gat[sub * 2 + t // 4, 12 + i // 2, pl.ds(i % 2 * 4 + t % 4, 1), :] = pts_v[i : i + 1, t * 128 : t * 128 + 128]
    loads[5].wait()
    req_v[sub] = jnp.zeros((1, 128), jnp.int32)
    req_v[sub, :, 0:8] = dfar_v[...]

    pl.semaphore_wait(barrier, NSUB + low_end + late * jnp.maximum(0, z - FAR_Z - EARLY + 1) + peers)

    def z_copy(source, target):
        return pltpu.make_async_remote_copy(
            table.at[core, source], table.at[core, source], z_send.at[target], z_recv.at[source],
            device_id=(target * 2 + core, sub), device_id_type=MESH,
        )

    def send_z(o, carry):
        z_copy(z, o).start()
        return carry

    def send_down(o, carry):
        pl.semaphore_signal(here_sem.at[z], inc=1, device_id=(o * 2 + core, sub), device_id_type=MESH)
        return send_z(o, carry)

    lax.fori_loop(0, low_end, send_down, 0)
    lax.fori_loop(EARLY, z - FAR_Z + 1, send_down, 0)

    def tell(o, carry):
        pl.semaphore_signal(step_sem, inc=1, device_id=(o * 2 + core, sub), device_id_type=MESH)
        return carry

    step = NEAR_Z - 1
    lax.fori_loop(jnp.where(z - step < EARLY, NZ, z - step), z - step + 1, tell, 0)
    lax.fori_loop(jnp.where(z < EARLY, NZ, z + step), jnp.minimum(NZ, z + step + 1), tell, 0)
    lax.fori_loop(near_from, z, send_z, 0)
    lax.fori_loop(near_next, near_end, send_z, 0)

    def half_copy(number, slot, target):
        return pltpu.make_async_remote_copy(
            gat.at[slot], gat.at[slot], gat_send.at[number], gat_recv.at[slot],
            device_id=(leaf, target), device_id_type=MESH,
        )

    sends = []

    def pass_on(half, d, steps):
        if d is None:
            slot, targets = sub * 2 + half, [at_plane(0, e) if half == 0 else at_plane(e, 0) for e in steps]
        else:
            origin = at_plane(0, d) if half == 0 else at_plane(d, 0)
            slot, targets = origin * 2 + half, [at_plane(e, 0) if half == 0 else at_plane(0, e) for e in steps]
            if d:
                half_copy(0, slot, origin).wait_recv()
        for target in targets:
            c = half_copy(len(sends), slot, target)
            c.start()
            sends.append(c)

    for d in (None, 0):
        for half in range(2):
            pass_on(half, d, (1, 3, 2))
    req_copies = []
    for i, o in enumerate(plane):
        req_copies.append(
            pltpu.make_async_remote_copy(
                req_v.at[sub], req_v.at[sub], req_send.at[i], req_recv.at[sub],
                device_id=(leaf, o), device_id_type=MESH,
            )
        )
    for c in req_copies:
        c.start()

    for i in range(9, 11):
        loads[i].wait()
    for given, to_h, to_l in ((dc_v, rd_h, rd_l), (gc_v, rg_h, rg_l)):
        high, low = split(given[...])
        given[...] = dot(high, perm_v[...], NN)
        for k in range(FAR):
            to_h[:, k * 128 : k * 128 + 128] = twice(stack(given[pl.ds(k, 32, stride=8), :])).astype(BF16)
        given[...] = dot(low, perm_v[...], NN)
        for k in range(FAR):
            to_l[:, k * 128 : k * 128 + 128] = twice(stack(given[pl.ds(k, 32, stride=8), :])).astype(BF16)
    for d in (1, 3):
        for half in range(2):
            pass_on(half, d, (1, 3, 2))
    told = (z - step >= EARLY).astype(jnp.int32) + late * (z + step < NZ).astype(jnp.int32)

    @pl.when(told > 0)
    def _():
        pl.semaphore_wait(step_sem, told)

    lax.fori_loop(mid_from, z - NEAR_Z + 1, send_z, 0)
    lax.fori_loop(mid_next, mid_end, send_z, 0)
    fw = dot3((rf_h[0:64, :], rf_l[0:64, :]), (w_h[...], w_l[...]), NN)
    fw_pair = split(fw)
    w_h[64:128, :] = fw_pair[0]
    w_l[64:128, :] = fw_pair[1]
    for t in range(LEAVES_DEV):
        for i in range(3):
            row = pts_v[i : i + 1, t * 128 : t * 128 + 128]
            cols_v[t, i] = jnp.broadcast_to(row, (128, 128)).T

    for half in range(2):
        pass_on(half, 2, (1, 3, 2))

    for i, o in enumerate(plane):
        pltpu.make_async_remote_copy(
            req_v.at[o], req_v.at[o], req_send.at[i], req_recv.at[o], device_id=(leaf, o), device_id_type=MESH
        ).wait_recv()
    to_scalar = pltpu.make_async_copy(req_v, req_s, req_loc)
    to_scalar.start()

    def send_up(o, carry):
        pl.semaphore_wait(here_sem.at[o], 1)
        return send_z(o, carry)

    def received(o, carry):
        z_copy(o, o).wait_recv()
        return carry

    lax.fori_loop(up_from, NZ, send_up, 0)
    lax.fori_loop(up_from, NZ, received, 0)
    lax.fori_loop(near_from, z, received, 0)
    lax.fori_loop(near_next, near_end, received, 0)
    lax.fori_loop(mid_from, z - NEAR_Z + 1, received, 0)
    lax.fori_loop(mid_next, mid_end, received, 0)
    lax.fori_loop(0, low_end, received, 0)
    lax.fori_loop(EARLY, z - FAR_Z + 1, received, 0)
    swap = pltpu.make_async_remote_copy(
        table.at[core], table.at[core], c_sem.at[0], c_sem.at[1], device_id=mate, device_id_type=MESH
    )
    swap.start()
    to_scalar.wait()
    for i in range(6, 9):
        loads[i].wait()
    pltpu.make_async_remote_copy(
        table.at[1 - core], table.at[1 - core], c_sem.at[0], c_sem.at[1], device_id=mate, device_id_type=MESH
    ).wait_recv()

    r_copies, p_copies = [], []
    pieces = []
    for k in range(FAR):
        number = gfar_s[0, k]
        pieces.append(spread(table[number & 1, number >> 1, 8:16, :]))
    part = pack(dot3(split(jnp.concatenate(pieces, axis=1)), (rg_h[...], rg_l[...]), NT))
    p_out[...] = part
    p_in[sub] = part
    for i, o in enumerate(plane):
        c = pltpu.make_async_remote_copy(
            p_out, p_in.at[sub], p_send.at[i], p_recv.at[sub], device_id=(leaf, o), device_id_type=MESH
        )
        c.start()
        p_copies.append(c)

    def answer(o, k):
        number = req_s[o, 0, k]
        row = table[(number >> 4) & 1, number >> 5, 0:8, :]
        return jnp.where(jnp.full((8, 128), number & (NSUB - 1), jnp.int32) == sub, row, 0.0)

    for i, o in enumerate(plane):
        for k in range(FAR):
            r_out[o, k] = answer(o, k)
        c = pltpu.make_async_remote_copy(
            r_out.at[o], r_in.at[sub], r_send.at[i], r_recv.at[sub], device_id=(leaf, o), device_id_type=MESH
        )
        c.start()
        r_copies.append(c)
    for k in range(FAR):
        r_in[sub, k] = answer(sub, k)
    for half in range(2):
        for d in range(NSUB):
            dy, dx = d // SIDE, d % SIDE
            if (dy if half == 0 else dx) == 0:
                continue
            slot = at_plane(dy, dx) * 2 + half
            pltpu.make_async_remote_copy(
                gat.at[slot], gat.at[slot], gat_send.at[0], gat_recv.at[slot], device_id=(leaf, sub), device_id_type=MESH
            ).wait_recv()
    loads[11].wait()

    def one_leaf(t, carry):
        total = jnp.zeros((16, 128), F32)
        for pair in range(NEAR // 2):
            tiles, vectors = [], []
            for k in (2 * pair, 2 * pair + 1):
                number = near_s[t, k]
                slot, j = number >> 2, number & 3
                square = DELTA_SQ
                for i in range(3):
                    along = cols_v[t, i] - gat[slot, 12 + i // 2, pl.ds(i % 2 * 4 + j, 1), :]
                    square = along * along + square
                tiles.append(lax.rsqrt(square))
                vectors.append(gat[slot, pl.ds(j * 2, 2)].reshape(16, 128))
            total = total + dot3(split(jnp.concatenate(vectors, axis=1)), split(jnp.concatenate(tiles, axis=1)), NT)
        lefts, rights = [], []
        for k in range(FAR):
            number = lfar_s[t, k]
            value = gat[number >> 2, 8 + (number & 3)]
            turned = pltpu.roll(value, 64, 1)
            lefts.append(jnp.concatenate([keep(0, value), keep(0, turned), keep(1, turned), keep(1, value)], axis=0))
            rights.append(lc_v[t, pl.ds(k, 32, stride=8), :])
        local = dot3(split(jnp.concatenate(lefts, axis=1)), split(jnp.concatenate(rights, axis=1)), NT)
        l_pair = split(local)
        field = NEAR_WEIGHT * total
        for parity in range(2):
            rows = slice(parity * 16, parity * 16 + 16)
            b_pair = split(basis_v[t, pl.ds(parity, 32, stride=2), :])
            field = field + dot3((l_pair[0][rows], l_pair[1][rows]), b_pair, NN)
        acc[t] = field
        return carry

    lax.fori_loop(0, LEAVES_DEV, one_leaf, 0)

    for i, o in enumerate(plane):
        pltpu.make_async_remote_copy(
            r_in.at[o], r_in.at[o], r_send.at[i], r_recv.at[o], device_id=(leaf, o), device_id_type=MESH
        ).wait_recv()
        pltpu.make_async_remote_copy(
            p_in.at[o], p_in.at[o], p_send.at[i], p_recv.at[o], device_id=(leaf, o), device_id_type=MESH
        ).wait_recv()
    asked = r_in[0]
    grp_local = p_in[0]
    for o in range(1, NSUB):
        asked = asked + r_in[o]
        grp_local = grp_local + p_in[o]
    dev_local = dot3(split(jnp.concatenate([spread(asked[k]) for k in range(FAR)], axis=1)), (rd_h[...], rd_l[...]), NT)
    both = split(jnp.where(left, dev_local, spread(grp_local)))
    far = dot3(both, (w_h[...], w_l[...]), NN)
    for t in range(LEAVES_DEV):
        field = acc[t] + far[:, t * 128 : t * 128 + 128]
        out[0, t] = field[0:8]
        out[1, t] = field[8:16]

    def sent(o, carry):
        z_copy(z, o).wait_send()
        return carry

    lax.fori_loop(0, z, sent, 0)
    lax.fori_loop(z + 1, NZ, sent, 0)
    for c in req_copies + sends + [swap] + r_copies + p_copies:
        c.wait_send()


def body(
    sources, points, basis, leaf_transfer, dev_transfer, leaf_coupling, dev_coupling, grp_coupling, near_list, leaf_far,
    dev_far, grp_far,
):
    def rows(array):
        m = array.shape[0]
        return array.reshape(m, 8, 32, 128).transpose(0, 2, 1, 3).reshape(m, 256, 128)

    in_hbm = pl.BlockSpec(memory_space=pltpu.HBM)
    vm, sm, dma = pltpu.VMEM, pltpu.SMEM, pltpu.SemaphoreType.DMA
    result = pl.pallas_call(
        kernel,
        out_shape=pltpu.VMEM((2, 8, 8, 128), F32),
        in_specs=[in_hbm] * 12,
        out_specs=pl.BlockSpec(memory_space=pltpu.VMEM),
        scratch_shapes=[
            vm((2, 8, 8, 128), F32), vm((3, 1024), F32), vm((8, 64, 128), F32), vm((256, 128), F32), vm((32, 128), F32),
            vm((8, 256, 128), F32), vm((256, 128), F32), vm((256, 128), F32), vm((1, 8), jnp.int32),
            sm((8, 8), jnp.int32), sm((8, 8), jnp.int32), sm((1, 8), jnp.int32),
            vm((128, 1024), BF16), vm((128, 1024), BF16), vm((128, 128), BF16), vm((128, 128), BF16),
            vm((128, 1024), BF16), vm((128, 1024), BF16), vm((128, 1024), BF16), vm((128, 1024), BF16),
            vm((128, 128), BF16), vm((8, 3, 128, 128), F32), vm((8, 16, 128), F32),
            vm((32, HALF_TILES, 8, 128), F32), vm((2, NZ, 16, 128), F32), vm((NSUB, 1, 128), jnp.int32), sm((NSUB, 1, 128), jnp.int32),
            vm((NSUB, FAR, 8, 128), F32), vm((NSUB, FAR, 8, 128), F32), vm((8, 128), F32), vm((NSUB, 8, 128), F32),
            dma((12,)), pltpu.SemaphoreType.REGULAR((NZ,)), pltpu.SemaphoreType.REGULAR, dma((30,)), dma((32,)), dma((16,)), dma((16,)), dma((2,)), dma((15,)), dma((16,)), dma,
            dma((15,)), dma((16,)), dma((15,)), dma((16,)),
        ],
        compiler_params=pltpu.CompilerParams(collective_id=0, has_side_effects=True, vmem_limit_bytes=60 * 1024 * 1024),
    )(
        sources.reshape(2, 8, 8, 128).transpose(0, 2, 1, 3),
        points,
        basis,
        rows(leaf_transfer[None])[0],
        dev_transfer.reshape(32, 128),
        rows(leaf_coupling),
        rows(dev_coupling)[0],
        rows(grp_coupling)[0],
        near_list, leaf_far, dev_far, grp_far,
    )
    return result.transpose(0, 2, 1, 3).reshape(16, 1024)


def solution(mesh):
    both = ("leaf", "sub")
    placed = (
        P(None, both), P(None, both), P(both, None, None), P(both, None), P(both, None), P(both, None, None),
        P(both, None, None), P("leaf", None, None), P(both, None), P(both, None), P(both, None), P("leaf", None),
    )
    return jax.shard_map(body, mesh=mesh, in_specs=placed, out_specs=P(None, both), check_vma=False)
```

```python
import jax
import jax.numpy as jnp
from jax import lax
from jax.experimental import pallas as pl
from jax.experimental.pallas import tpu as pltpu
from jax.sharding import PartitionSpec as P

MESH = pl.DeviceIdType.MESH
F32, BF16 = jnp.float32, jnp.bfloat16
DELTA_SQ = 0.01
NZ, NSUB, SIDE = 16, 16, 4
EARLY, FAR_Z, NEAR_Z = 6, 9, 5
LEAVES_DEV, NEAR, FAR = 8, 8, 8
HALF_TILES = 14
NEAR_WEIGHT = 1.0 / 32.0
NT = ((1,), (1,))
NN = ((1,), (0,))


def split(x):
    high = x.astype(BF16)
    return high, (x - high.astype(F32)).astype(BF16)


def dot(a, b, dims):
    return lax.dot_general(a, b, (dims, ((), ())), preferred_element_type=F32)


def dot3(a, b, dims):
    m = a[0].shape[0]
    both = dot(jnp.concatenate(a, axis=0), b[0], dims)
    return both[:m] + (both[m:] + dot(a[0], b[1], dims))


def kernel(
    src, pts, basis, e_hbm, f_hbm, lc_hbm, dc_hbm, gc_hbm, near_hbm, lfar_hbm, dfar_hbm, gfar_hbm,
    out,
    src_v, pts_v, basis_v, e_v, f_v, lc_v, dc_v, gc_v, dfar_v, near_s, lfar_s, gfar_s,
    w_h, w_l, rf_h, rf_l, rd_h, rd_l, rg_h, rg_l, perm_v, cols_v, acc,
    gat, table, req_v, req_s, r_out, r_in, p_out, p_in,
    loc_sem, here_sem, step_sem, gat_send, gat_recv, z_send, z_recv, c_sem, req_send, req_recv, req_loc, r_send, r_recv, p_send, p_recv,
):
    leaf = lax.axis_index("leaf")
    sub = lax.axis_index("sub")
    z, core = leaf // 2, lax.rem(leaf, 2)
    y, x = sub // SIDE, lax.rem(sub, SIDE)

    def at_plane(dy, dx):
        return lax.rem(y + dy, SIDE) * SIDE + lax.rem(x + dx, SIDE)

    ring = (0, 1, 2, 1)
    order = sorted(range(1, NSUB), key=lambda d: -ring[d // SIDE] - ring[d % SIDE])
    plane = [at_plane(d // SIDE, d % SIDE) for d in order]
    late = (z >= EARLY).astype(jnp.int32)
    up_from = jnp.where(z < EARLY, z + 1, z + FAR_Z)
    low_end = jnp.minimum(z, EARLY)
    near_from = jnp.maximum(EARLY, z - NEAR_Z + 1)
    near_next = jnp.where(z < EARLY, NZ, z + 1)
    near_end = jnp.minimum(NZ, z + NEAR_Z)
    mid_from = jnp.maximum(EARLY, z - FAR_Z + 1)
    mid_next = jnp.where(z < EARLY, NZ, z + NEAR_Z)
    mid_end = jnp.minimum(NZ, z + FAR_Z)
    peers = late * (near_end - 1 - near_from)

    mate = (leaf + 1 - 2 * core, sub)

    barrier = pltpu.get_barrier_semaphore()
    for o in plane:
        pl.semaphore_signal(barrier, inc=1, device_id=(leaf, o), device_id_type=MESH)
    pl.semaphore_signal(barrier, inc=1, device_id=mate, device_id_type=MESH)

    def announce(o, carry):
        pl.semaphore_signal(barrier, inc=1, device_id=(o * 2 + core, sub), device_id_type=MESH)
        return carry

    lax.fori_loop(near_from, z, announce, 0)
    lax.fori_loop(near_next, near_end, announce, 0)
    lax.fori_loop(up_from, NZ, announce, 0)

    pairs = [
        (basis, basis_v), (e_hbm, e_v), (src, src_v), (f_hbm, f_v), (pts, pts_v), (dfar_hbm, dfar_v), (near_hbm, near_s),
        (lfar_hbm, lfar_s), (gfar_hbm, gfar_s), (dc_hbm, dc_v), (gc_hbm, gc_v), (lc_hbm, lc_v),
    ]
    loads = [pltpu.make_async_copy(a, b, loc_sem.at[i]) for i, (a, b) in enumerate(pairs)]
    for c in loads:
        c.start()
    lane = lax.broadcasted_iota(jnp.int32, (1, 128), 1)
    left = lane < 64

    def keep(part, value):
        return jnp.where(left if part == 0 else jnp.logical_not(left), value, 0.0)

    def stack(value):
        return jnp.concatenate([keep(0, value), keep(1, value)], axis=0)

    def twice(value):
        return jnp.concatenate([value, value], axis=0)

    def pack(value):
        return jnp.where(left, value[0:8], value[8:16])

    def spread(value):
        turned = pltpu.roll(value, 64, 1)
        return jnp.concatenate([jnp.where(left, value, turned), jnp.where(left, turned, value)], axis=0)

    row_i = lax.broadcasted_iota(jnp.int32, (128, 128), 0)
    col_i = lax.broadcasted_iota(jnp.int32, (128, 128), 1)
    wanted = (col_i // 64) * 64 + 2 * lax.rem(col_i, 32) + lax.rem(col_i // 32, 2)
    perm_v[...] = (row_i == wanted).astype(F32).astype(BF16)

    for i in range(4):
        loads[i].wait()
    for t in range(LEAVES_DEV):
        lanes = pl.ds(t * 128, 128)
        e_pair = split(stack(e_v[pl.ds(t, 32, stride=8), :]))
        b_pair = split(twice(basis_v[t]))
        w_pair = split(dot3(e_pair, b_pair, NN))
        for k in range(2):
            w_h[pl.ds(k * 64, 64), lanes] = w_pair[0]
            w_l[pl.ds(k * 64, 64), lanes] = w_pair[1]
    signal = [jnp.concatenate([src_v[0, t], src_v[1, t]], axis=0) for t in range(LEAVES_DEV)]
    s_pair = split(jnp.concatenate(signal, axis=1))
    dev_coef = dot3(s_pair, (w_h[...], w_l[...]), NT)
    f_high, f_low = split(f_v[...])
    f_high, f_low = dot(f_high, perm_v[...], NN), dot(f_low, perm_v[...], NN)
    rf_h[...] = twice(stack(f_high)).astype(BF16)
    rf_l[...] = twice(stack(f_low)).astype(BF16)
    d_pair = split(jnp.where(left, dev_coef, 0.0) + jnp.where(left, 0.0, dev_coef))
    up = dot3(d_pair, (rf_h[...], rf_l[...]), NT)
    table[core, z, 0:8, :] = pack(dev_coef)
    table[core, z, 8:16, :] = pack(up)
    loads[4].wait()
    for t in range(LEAVES_DEV):
        slot, j = sub * 2 + t // 4, t % 4
        b_pair = split(twice(basis_v[t]))
        t_pair = (s_pair[0][:, t * 128 : t * 128 + 128], s_pair[1][:, t * 128 : t * 128 + 128])
        gat[slot, 2 * j] = src_v[0, t]
        gat[slot, 2 * j + 1] = src_v[1, t]
        gat[slot, 8 + j] = pack(dot3(t_pair, b_pair, NT))
    for half in range(2):
        gat[sub * 2 + half, 13] = jnp.zeros((8, 128), F32)
    for t in range(LEAVES_DEV):
        for i in range(3):
            gat[sub * 2 + t // 4, 12 + i // 2, pl.ds(i % 2 * 4 + t % 4, 1), :] = pts_v[i : i + 1, t * 128 : t * 128 + 128]
    loads[5].wait()
    req_v[sub] = jnp.zeros((1, 128), jnp.int32)
    req_v[sub, :, 0:8] = dfar_v[...]

    pl.semaphore_wait(barrier, NSUB + low_end + late * jnp.maximum(0, z - FAR_Z - EARLY + 1) + peers)

    def z_copy(source, target):
        return pltpu.make_async_remote_copy(
            table.at[core, source], table.at[core, source], z_send.at[target], z_recv.at[source],
            device_id=(target * 2 + core, sub), device_id_type=MESH,
        )

    def send_z(o, carry):
        z_copy(z, o).start()
        return carry

    def send_down(o, carry):
        pl.semaphore_signal(here_sem.at[z], inc=1, device_id=(o * 2 + core, sub), device_id_type=MESH)
        return send_z(o, carry)

    lax.fori_loop(0, low_end, send_down, 0)
    lax.fori_loop(EARLY, z - FAR_Z + 1, send_down, 0)

    def tell(o, carry):
        pl.semaphore_signal(step_sem, inc=1, device_id=(o * 2 + core, sub), device_id_type=MESH)
        return carry

    step = NEAR_Z - 1
    lax.fori_loop(jnp.where(z - step < EARLY, NZ, z - step), z - step + 1, tell, 0)
    lax.fori_loop(jnp.where(z < EARLY, NZ, z + step), jnp.minimum(NZ, z + step + 1), tell, 0)
    lax.fori_loop(near_from, z, send_z, 0)
    lax.fori_loop(near_next, near_end, send_z, 0)

    def half_copy(number, slot, target):
        return pltpu.make_async_remote_copy(
            gat.at[slot], gat.at[slot], gat_send.at[number], gat_recv.at[slot],
            device_id=(leaf, target), device_id_type=MESH,
        )

    sends = []

    def pass_on(half, d, steps):
        if d is None:
            slot, targets = sub * 2 + half, [at_plane(0, e) if half == 0 else at_plane(e, 0) for e in steps]
        else:
            origin = at_plane(0, d) if half == 0 else at_plane(d, 0)
            slot, targets = origin * 2 + half, [at_plane(e, 0) if half == 0 else at_plane(0, e) for e in steps]
            if d:
                half_copy(0, slot, origin).wait_recv()
        for target in targets:
            c = half_copy(len(sends), slot, target)
            c.start()
            sends.append(c)

    for d in (None, 0):
        for half in range(2):
            pass_on(half, d, (1, 3, 2))
    req_copies = []
    for i, o in enumerate(plane):
        req_copies.append(
            pltpu.make_async_remote_copy(
                req_v.at[sub], req_v.at[sub], req_send.at[i], req_recv.at[sub],
                device_id=(leaf, o), device_id_type=MESH,
            )
        )
    for c in req_copies:
        c.start()

    for i in range(9, 11):
        loads[i].wait()
    for given, to_h, to_l in ((dc_v, rd_h, rd_l), (gc_v, rg_h, rg_l)):
        high, low = split(given[...])
        given[...] = dot(high, perm_v[...], NN)
        for k in range(FAR):
            to_h[:, k * 128 : k * 128 + 128] = twice(stack(given[pl.ds(k, 32, stride=8), :])).astype(BF16)
        given[...] = dot(low, perm_v[...], NN)
        for k in range(FAR):
            to_l[:, k * 128 : k * 128 + 128] = twice(stack(given[pl.ds(k, 32, stride=8), :])).astype(BF16)
    for d in (1, 3):
        for half in range(2):
            pass_on(half, d, (1, 3, 2))
    told = (z - step >= EARLY).astype(jnp.int32) + late * (z + step < NZ).astype(jnp.int32)

    @pl.when(told > 0)
    def _():
        pl.semaphore_wait(step_sem, told)

    lax.fori_loop(mid_from, z - NEAR_Z + 1, send_z, 0)
    lax.fori_loop(mid_next, mid_end, send_z, 0)
    fw = dot3((rf_h[0:64, :], rf_l[0:64, :]), (w_h[...], w_l[...]), NN)
    fw_pair = split(fw)
    w_h[64:128, :] = fw_pair[0]
    w_l[64:128, :] = fw_pair[1]
    for t in range(LEAVES_DEV):
        for i in range(3):
            row = pts_v[i : i + 1, t * 128 : t * 128 + 128]
            cols_v[t, i] = jnp.broadcast_to(row, (128, 128)).T

    for half in range(2):
        pass_on(half, 2, (1, 3, 2))

    for i, o in enumerate(plane):
        pltpu.make_async_remote_copy(
            req_v.at[o], req_v.at[o], req_send.at[i], req_recv.at[o], device_id=(leaf, o), device_id_type=MESH
        ).wait_recv()
    to_scalar = pltpu.make_async_copy(req_v, req_s, req_loc)
    to_scalar.start()

    def send_up(o, carry):
        pl.semaphore_wait(here_sem.at[o], 1)
        return send_z(o, carry)

    def received(o, carry):
        z_copy(o, o).wait_recv()
        return carry

    lax.fori_loop(up_from, NZ, send_up, 0)
    lax.fori_loop(up_from, NZ, received, 0)
    lax.fori_loop(near_from, z, received, 0)
    lax.fori_loop(near_next, near_end, received, 0)
    lax.fori_loop(mid_from, z - NEAR_Z + 1, received, 0)
    lax.fori_loop(mid_next, mid_end, received, 0)
    lax.fori_loop(0, low_end, received, 0)
    lax.fori_loop(EARLY, z - FAR_Z + 1, received, 0)
    swap = pltpu.make_async_remote_copy(
        table.at[core], table.at[core], c_sem.at[0], c_sem.at[1], device_id=mate, device_id_type=MESH
    )
    swap.start()
    to_scalar.wait()
    for i in range(6, 9):
        loads[i].wait()
    pltpu.make_async_remote_copy(
        table.at[1 - core], table.at[1 - core], c_sem.at[0], c_sem.at[1], device_id=mate, device_id_type=MESH
    ).wait_recv()

    r_copies, p_copies = [], []
    pieces = []
    for k in range(FAR):
        number = gfar_s[0, k]
        pieces.append(spread(table[number & 1, number >> 1, 8:16, :]))
    part = pack(dot3(split(jnp.concatenate(pieces, axis=1)), (rg_h[...], rg_l[...]), NT))
    p_out[...] = part
    p_in[sub] = part
    for i, o in enumerate(plane):
        c = pltpu.make_async_remote_copy(
            p_out, p_in.at[sub], p_send.at[i], p_recv.at[sub], device_id=(leaf, o), device_id_type=MESH
        )
        c.start()
        p_copies.append(c)

    def answer(o, k):
        number = req_s[o, 0, k]
        row = table[(number >> 4) & 1, number >> 5, 0:8, :]
        return jnp.where(jnp.full((8, 128), number & (NSUB - 1), jnp.int32) == sub, row, 0.0)

    for i, o in enumerate(plane):
        for k in range(FAR):
            r_out[o, k] = answer(o, k)
        c = pltpu.make_async_remote_copy(
            r_out.at[o], r_in.at[sub], r_send.at[i], r_recv.at[sub], device_id=(leaf, o), device_id_type=MESH
        )
        c.start()
        r_copies.append(c)
    for k in range(FAR):
        r_in[sub, k] = answer(sub, k)
    for half in range(2):
        for d in range(NSUB):
            dy, dx = d // SIDE, d % SIDE
            if (dy if half == 0 else dx) == 0:
                continue
            slot = at_plane(dy, dx) * 2 + half
            pltpu.make_async_remote_copy(
                gat.at[slot], gat.at[slot], gat_send.at[0], gat_recv.at[slot], device_id=(leaf, sub), device_id_type=MESH
            ).wait_recv()
    loads[11].wait()

    def one_leaf(t, carry):
        total = jnp.zeros((16, 128), F32)
        for pair in range(NEAR // 2):
            tiles, vectors = [], []
            for k in (2 * pair, 2 * pair + 1):
                number = near_s[t, k]
                slot, j = number >> 2, number & 3
                square = DELTA_SQ
                for i in range(3):
                    along = cols_v[t, i] - gat[slot, 12 + i // 2, pl.ds(i % 2 * 4 + j, 1), :]
                    square = along * along + square
                tiles.append(lax.rsqrt(square))
                vectors.append(gat[slot, pl.ds(j * 2, 2)].reshape(16, 128))
            total = total + dot3(split(jnp.concatenate(vectors, axis=1)), split(jnp.concatenate(tiles, axis=1)), NT)
        lefts, rights = [], []
        for k in range(FAR):
            number = lfar_s[t, k]
            value = gat[number >> 2, 8 + (number & 3)]
            turned = pltpu.roll(value, 64, 1)
            lefts.append(jnp.concatenate([keep(0, value), keep(0, turned), keep(1, turned), keep(1, value)], axis=0))
            rights.append(lc_v[t, pl.ds(k, 32, stride=8), :])
        local = dot3(split(jnp.concatenate(lefts, axis=1)), split(jnp.concatenate(rights, axis=1)), NT)
        l_pair = split(local)
        field = NEAR_WEIGHT * total
        for parity in range(2):
            rows = slice(parity * 16, parity * 16 + 16)
            b_pair = split(basis_v[t, pl.ds(parity, 32, stride=2), :])
            field = field + dot3((l_pair[0][rows], l_pair[1][rows]), b_pair, NN)
        acc[t] = field
        return carry

    lax.fori_loop(0, LEAVES_DEV, one_leaf, 0)

    for i, o in enumerate(plane):
        pltpu.make_async_remote_copy(
            r_in.at[o], r_in.at[o], r_send.at[i], r_recv.at[o], device_id=(leaf, o), device_id_type=MESH
        ).wait_recv()
        pltpu.make_async_remote_copy(
            p_in.at[o], p_in.at[o], p_send.at[i], p_recv.at[o], device_id=(leaf, o), device_id_type=MESH
        ).wait_recv()
    asked = r_in[0]
    grp_local = p_in[0]
    for o in range(1, NSUB):
        asked = asked + r_in[o]
        grp_local = grp_local + p_in[o]
    dev_local = dot3(split(jnp.concatenate([spread(asked[k]) for k in range(FAR)], axis=1)), (rd_h[...], rd_l[...]), NT)
    both = split(jnp.where(left, dev_local, spread(grp_local)))
    far = dot3(both, (w_h[...], w_l[...]), NN)
    for t in range(LEAVES_DEV):
        field = acc[t] + far[:, t * 128 : t * 128 + 128]
        out[0, t] = field[0:8]
        out[1, t] = field[8:16]

    def sent(o, carry):
        z_copy(z, o).wait_send()
        return carry

    lax.fori_loop(0, z, sent, 0)
    lax.fori_loop(z + 1, NZ, sent, 0)
    for c in req_copies + sends + [swap] + r_copies + p_copies:
        c.wait_send()


def body(
    sources, points, basis, leaf_transfer, dev_transfer, leaf_coupling, dev_coupling, grp_coupling, near_list, leaf_far,
    dev_far, grp_far,
):
    def rows(array):
        m = array.shape[0]
        return array.reshape(m, 8, 32, 128).transpose(0, 2, 1, 3).reshape(m, 256, 128)

    in_hbm = pl.BlockSpec(memory_space=pltpu.HBM)
    vm, sm, dma = pltpu.VMEM, pltpu.SMEM, pltpu.SemaphoreType.DMA
    result = pl.pallas_call(
        kernel,
        out_shape=pltpu.VMEM((2, 8, 8, 128), F32),
        in_specs=[in_hbm] * 12,
        out_specs=pl.BlockSpec(memory_space=pltpu.VMEM),
        scratch_shapes=[
            vm((2, 8, 8, 128), F32), vm((3, 1024), F32), vm((8, 64, 128), F32), vm((256, 128), F32), vm((32, 128), F32),
            vm((8, 256, 128), F32), vm((256, 128), F32), vm((256, 128), F32), vm((1, 8), jnp.int32),
            sm((8, 8), jnp.int32), sm((8, 8), jnp.int32), sm((1, 8), jnp.int32),
            vm((128, 1024), BF16), vm((128, 1024), BF16), vm((128, 128), BF16), vm((128, 128), BF16),
            vm((128, 1024), BF16), vm((128, 1024), BF16), vm((128, 1024), BF16), vm((128, 1024), BF16),
            vm((128, 128), BF16), vm((8, 3, 128, 128), F32), vm((8, 16, 128), F32),
            vm((32, HALF_TILES, 8, 128), F32), vm((2, NZ, 16, 128), F32), vm((NSUB, 1, 128), jnp.int32), sm((NSUB, 1, 128), jnp.int32),
            vm((NSUB, FAR, 8, 128), F32), vm((NSUB, FAR, 8, 128), F32), vm((8, 128), F32), vm((NSUB, 8, 128), F32),
            dma((12,)), pltpu.SemaphoreType.REGULAR((NZ,)), pltpu.SemaphoreType.REGULAR, dma((30,)), dma((32,)), dma((16,)), dma((16,)), dma((2,)), dma((15,)), dma((16,)), dma,
            dma((15,)), dma((16,)), dma((15,)), dma((16,)),
        ],
        compiler_params=pltpu.CompilerParams(collective_id=0, has_side_effects=True, vmem_limit_bytes=60 * 1024 * 1024),
    )(
        sources.reshape(2, 8, 8, 128).transpose(0, 2, 1, 3),
        points,
        basis,
        rows(leaf_transfer[None])[0],
        dev_transfer.reshape(32, 128),
        rows(leaf_coupling),
        rows(dev_coupling)[0],
        rows(grp_coupling)[0],
        near_list, leaf_far, dev_far, grp_far,
    )
    return result.transpose(0, 2, 1, 3).reshape(16, 1024)


def solution(mesh):
    both = ("leaf", "sub")
    placed = (
        P(None, both), P(None, both), P(both, None, None), P(both, None), P(both, None), P(both, None, None),
        P(both, None, None), P("leaf", None, None), P(both, None), P(both, None), P(both, None), P("leaf", None),
    )
    return jax.shard_map(body, mesh=mesh, in_specs=placed, out_specs=P(None, both), check_vma=False)
```
